32 devices in a mesh: head: 4 (over y, x), seq: 8 (over z, core).
Axes of the slice: x: 2, y: 2, z: 4, core: 2. Of those that a mesh axis runs over, the one named last changes fastest.
Arguments:
- queries: bfloat16 [8, 512, 4096], P('seq', 'head'), may hold values from -13 to 13
- keys: bfloat16 [8, 512, 1024], P('seq', 'head'), may hold values from -8 to 8
- values: bfloat16 [8, 512, 1024], P('seq', 'head'), may hold values from -6 to 6
- output_gradient: bfloat16 [8, 512, 4096], P('seq', 'head'), may hold values from -6 to 6
- windows: int32 [32], replicated, may hold values from 1 to 4, as said below
- sinks: int32 [32], replicated, may hold values from 0 to 2, as said below
Outputs:
- grad_queries: bfloat16 [8, 512, 4096], P('seq', 'head')
- key_gradient: bfloat16 [8, 512, 1024], P('seq', 'head')
- value_gradient: bfloat16 [8, 512, 1024], P('seq', 'head')
The draws below stay inside these ranges and needn't reach their ends.
Inputs may be any that keep to these rules, and one draw needn't show every extreme that they name: `windows`: some head has a window of exactly 4 blocks. `sinks`: some head has exactly 2 sink blocks.
All inputs are finite; a program needn't handle non-finite values.
Results may differ from the reference program's by a relative error of at most 0.009.
Values may be sent and summed in bfloat16 or wider, within the bound.
A program may use at most 64 MiB of HBM per device.

```python
import math
import jax
import jax.numpy as jnp
from jax import lax

QUERY_HEADS = 32
KEY_VALUE_HEADS = 8
HEAD_DIMENSION = 128
BLOCK_TOKENS = 128
WMAX = 4
SMAX = 2
SPAN_COUNT = 8
SPAN_LENGTH = 512


def build_keys(key):
    full_rows = SPAN_COUNT * SPAN_LENGTH
    starting_rows = jnp.clip(jax.random.normal(jax.random.fold_in(key, 11), (full_rows, KEY_VALUE_HEADS * HEAD_DIMENSION), jnp.float32), -6.0, 6.0)
    return starting_rows


def draw_keys(key, part):
    return build_keys(key).reshape(SPAN_COUNT, SPAN_LENGTH, KEY_VALUE_HEADS * HEAD_DIMENSION).astype(jnp.bfloat16)


def draw_queries(key, part):
    full_rows = SPAN_COUNT * SPAN_LENGTH
    drawn_rows = jnp.clip(jax.random.normal(jax.random.fold_in(key, 13), (full_rows, QUERY_HEADS * HEAD_DIMENSION), jnp.float32), -6.0, 6.0)
    return drawn_rows.reshape(SPAN_COUNT, SPAN_LENGTH, QUERY_HEADS * HEAD_DIMENSION).astype(jnp.bfloat16)


def draw_windows(key, part):
    raw_counts = jax.random.randint(jax.random.fold_in(key, 21), (QUERY_HEADS,), 1, WMAX + 1)
    picked = jax.random.randint(jax.random.fold_in(key, 22), (), 0, QUERY_HEADS)
    return jnp.where(jnp.arange(QUERY_HEADS) == picked, WMAX, raw_counts).astype(jnp.int32)


def draw_sinks(key, part):
    raw_counts = jax.random.randint(jax.random.fold_in(key, 31), (QUERY_HEADS,), 0, SMAX + 1)
    picked = jax.random.randint(jax.random.fold_in(key, 32), (), 0, QUERY_HEADS)
    return jnp.where(jnp.arange(QUERY_HEADS) == picked, SMAX, raw_counts).astype(jnp.int32)


def shard_levels(stream_key, shape, shards, smallest, largest):
    def one(dim, parts):
        draws = jax.random.uniform(jax.random.fold_in(jax.random.fold_in(stream_key, 6), dim), (parts,), jnp.float32, smallest / len(shards), largest / len(shards))
        return jnp.repeat(jnp.exp(draws), shape[dim] // parts).reshape((-1,) + (1,) * (len(shape) - dim - 1))

    factor_of = one(*shards[0])
    for cut in shards[1:]:
        factor_of = factor_of * one(*cut)
    return factor_of


def centred(rng, dims, width, reach, split=(), kind=jnp.bfloat16):
    values = jax.random.normal(rng, dims, jnp.float32) * width
    if len(split) > 0:
        values = shard_levels(rng, dims, split, -0.22, 0.18) * values
    return jnp.clip(values, min=-reach, max=reach).astype(kind)


def setup_inputs(seed: int = 0) -> dict:
    seeds = jax.random.split(jax.random.key(seed), 7)
    return {
        "queries": draw_queries(jax.random.fold_in(seeds[6], 71), 0),
        "keys": draw_keys(jax.random.fold_in(seeds[6], 71), 0),
        "values": centred(seeds[2], (SPAN_COUNT, SPAN_LENGTH, KEY_VALUE_HEADS * HEAD_DIMENSION), 1.0, 6.0, ((0, 8), (1, 4))),
        "output_gradient": centred(seeds[3], (SPAN_COUNT, SPAN_LENGTH, QUERY_HEADS * HEAD_DIMENSION), 1.0, 6.0, ((0, 8), (1, 4))),
        "windows": draw_windows(jax.random.fold_in(seeds[6], 71), 0),
        "sinks": draw_sinks(jax.random.fold_in(seeds[6], 71), 0),
    }


NEG_FILL = -1e+30

def mask_for(query_blocks, window, sink_count, block, wmax, smax):
    columns = jnp.arange((wmax + smax) * block, dtype=jnp.int32)
    slot_id = columns // block
    col_tok = columns % block
    row_tok = jnp.arange(block, dtype=jnp.int32)
    query_block = query_blocks.reshape((-1,) + (1,) * (window.ndim + 2))
    win_w = window[None, ..., None, None]
    sink_s = sink_count[None, ..., None, None]
    in_window = slot_id < wmax
    causal = (slot_id > 0) | (col_tok[None, :] <= row_tok[:, None])
    window_ok = in_window & (query_block - slot_id >= 0) & (slot_id < win_w) & causal
    sink_ok = jnp.logical_not(in_window) & (slot_id - wmax < sink_s) & (slot_id - wmax <= query_block - win_w)
    return window_ok | sink_ok

def slot_keys(padded, whole, block_count):
    windowed = jnp.stack([padded[WMAX - 1 - offset:WMAX - 1 - offset + block_count] for offset in range(WMAX)], 1)
    sunk = jnp.broadcast_to(whole[:SMAX][None], (block_count, SMAX, BLOCK_TOKENS, HEAD_DIMENSION))
    joined = jnp.concatenate([windowed, sunk], 1)
    return joined.reshape(block_count, (WMAX + SMAX) * BLOCK_TOKENS, HEAD_DIMENSION).astype(jnp.float32)

def fold_slots(slot_grads, block_count):
    parts_all = slot_grads.reshape(block_count, WMAX + SMAX, BLOCK_TOKENS, HEAD_DIMENSION)
    total = jnp.zeros((block_count + WMAX - 1, BLOCK_TOKENS, HEAD_DIMENSION), jnp.float32)
    for offset in range(WMAX):
        total = total.at[WMAX - 1 - offset:WMAX - 1 - offset + block_count].add(parts_all[:, offset])
    total = total[WMAX - 1:]
    return total.at[:SMAX].add(lax.optimization_barrier(jnp.sum(parts_all[:, WMAX:], 0)))

def head_grads(q_head, go_head, k_head, v_head, window, sink_count):
    block_count = q_head.shape[0]
    scale_factor = 1.0 / math.sqrt(HEAD_DIMENSION)
    zero_pad = jnp.zeros((WMAX - 1, BLOCK_TOKENS, HEAD_DIMENSION), k_head.dtype)
    key_collection = slot_keys(jnp.concatenate([zero_pad, k_head], 0), k_head, block_count)
    value_collection = slot_keys(jnp.concatenate([zero_pad, v_head], 0), v_head, block_count)
    allowed = mask_for(jnp.arange(block_count, dtype=jnp.int32), window, sink_count, BLOCK_TOKENS, WMAX, SMAX)
    query_wide = q_head.astype(jnp.float32)
    output_grad_wide = go_head.astype(jnp.float32)
    score_matrix = jnp.einsum('frx,fpx->frp', query_wide, key_collection) * scale_factor
    score_matrix = jnp.where(allowed, score_matrix, NEG_FILL)
    row_max = lax.optimization_barrier(jnp.max(score_matrix, -1, keepdims=True))
    exp_scores = jnp.exp(score_matrix - row_max)
    weights = exp_scores / lax.optimization_barrier(jnp.sum(exp_scores, -1, keepdims=True))
    block_weights = lax.optimization_barrier(weights.astype(jnp.bfloat16)).astype(jnp.float32)
    attention_output = jnp.einsum('eng,egv->env', block_weights, value_collection)
    row_dot = lax.optimization_barrier(jnp.sum(output_grad_wide * attention_output, -1, keepdims=True))
    weight_gradient = jnp.einsum('frx,fpx->frp', output_grad_wide, value_collection)
    score_block_grad = (weights * (weight_gradient - row_dot)).astype(jnp.bfloat16)
    score_block_grad = lax.optimization_barrier(score_block_grad).astype(jnp.float32)
    query_grad_result = jnp.einsum('eng,egv->env', score_block_grad, key_collection) * scale_factor
    key_grad_result = jnp.einsum('nze,nzp->nep', score_block_grad, query_wide) * scale_factor
    value_grad_result = jnp.einsum('nze,nzp->nep', block_weights, output_grad_wide)
    return (query_grad_result, fold_slots(key_grad_result, block_count), fold_slots(value_grad_result, block_count))

def reference(queries, keys, values, output_gradient, windows, sinks):
    block_count = SPAN_COUNT * SPAN_LENGTH // BLOCK_TOKENS
    group_width = QUERY_HEADS // KEY_VALUE_HEADS
    query_full = queries.reshape(block_count, BLOCK_TOKENS, KEY_VALUE_HEADS, group_width, HEAD_DIMENSION).transpose(2, 3, 0, 1, 4)
    output_grad_full = output_gradient.reshape(block_count, BLOCK_TOKENS, KEY_VALUE_HEADS, group_width, HEAD_DIMENSION).transpose(2, 3, 0, 1, 4)
    key_full = keys.reshape(block_count, BLOCK_TOKENS, KEY_VALUE_HEADS, HEAD_DIMENSION).transpose(2, 0, 1, 3)
    value_full = values.reshape(block_count, BLOCK_TOKENS, KEY_VALUE_HEADS, HEAD_DIMENSION).transpose(2, 0, 1, 3)
    window_lookup = windows.reshape(KEY_VALUE_HEADS, group_width)
    sink_lookup = sinks.reshape(KEY_VALUE_HEADS, group_width)

    def per_kv_head(head_items):
        q_grp, g_grp, k_head, v_head, win_grp, sink_grp = head_items

        def per_q_head(running, inner_items):
            q_head, go_head, window, sink_count = inner_items
            query_grad_result, key_grad_result, value_grad_result = head_grads(q_head, go_head, k_head, v_head, window, sink_count)
            return ((running[0] + key_grad_result, running[1] + value_grad_result), query_grad_result)
        zero_grads = jnp.zeros((block_count, BLOCK_TOKENS, HEAD_DIMENSION), jnp.float32)
        (key_grad_result, value_grad_result), query_grad_result = lax.scan(per_q_head, (zero_grads, zero_grads), (q_grp, g_grp, win_grp, sink_grp))
        return (query_grad_result, key_grad_result, value_grad_result)
    query_grad_result, key_grad_result, value_grad_result = lax.map(per_kv_head, (query_full, output_grad_full, key_full, value_full, window_lookup, sink_lookup))
    grad_queries = query_grad_result.transpose(2, 3, 0, 1, 4).reshape(SPAN_COUNT, SPAN_LENGTH, QUERY_HEADS * HEAD_DIMENSION).astype(jnp.bfloat16)
    key_gradient = key_grad_result.transpose(1, 2, 0, 3).reshape(SPAN_COUNT, SPAN_LENGTH, KEY_VALUE_HEADS * HEAD_DIMENSION).astype(jnp.bfloat16)
    value_gradient = value_grad_result.transpose(1, 2, 0, 3).reshape(SPAN_COUNT, SPAN_LENGTH, KEY_VALUE_HEADS * HEAD_DIMENSION).astype(jnp.bfloat16)
    return (grad_queries, key_gradient, value_gradient)
```

```python
import functools
import math

import jax
import jax.numpy as jnp
from jax import lax
from jax.experimental import pallas as pl
from jax.experimental.pallas import tpu as pltpu
from jax.sharding import PartitionSpec as P

QUERY_HEADS = 32
KEY_VALUE_HEADS = 8
HEAD_DIMENSION = 128
BLOCK_TOKENS = 128
WMAX = 4
SMAX = 2

NEG_FILL = -1e30
GROUP = QUERY_HEADS // KEY_VALUE_HEADS
BACK = WMAX - 1
LOOK = 2
MESH = pl.DeviceIdType.MESH


def spare_links(head_count):
    return [
        (h, c)
        for c in range(SMAX)
        for h in range(head_count)
        if h != c and not 1 <= h - c <= BACK
    ]


def kernel(
    head_count,
    seq_count,
    q_ref, k_ref, v_ref, go_ref, win_ref, sink_ref,
    dq_ref, dk_ref, dv_ref,
    own, window, sunk, gsend, grecv, rsend, rrecv, gown, rpart, yrecv,
    w_send, w_recv, s_send, s_recv, x_send, x_recv,
    g_send, g_recv, r_send, r_recv, y_send, y_recv,
):
    G = KEY_VALUE_HEADS
    D = HEAD_DIMENSION
    T = BLOCK_TOKENS
    head = lax.axis_index("head")
    seq = lax.axis_index("seq")
    total = head_count * seq_count
    b = seq * head_count + head
    even = lax.rem(seq, 2) == 0
    first = seq == 0
    scale = 1.0 / math.sqrt(D)
    spare = spare_links(head_count)

    def device(block):
        return {"head": lax.rem(block + total, total) % head_count,
                "seq": lax.div(lax.rem(block + total, total), head_count)}

    def in_seq(s):
        return {"head": head, "seq": lax.rem(s + 2 * seq_count, seq_count)}

    def in_first(h):
        return {"head": h, "seq": 0}

    def remote(src, dst, ssem, rsem, where):
        return pltpu.make_async_remote_copy(
            src_ref=src, dst_ref=dst, send_sem=ssem, recv_sem=rsem,
            device_id=where, device_id_type=MESH)

    partners = []
    for d in range(1, BACK + 1):
        partners.append((b + d < total, device(b + d)))
        partners.append((b >= d, device(b - d)))
    to_core = even & (seq + 1 < seq_count)
    to_next = even & (seq + 2 < seq_count)
    from_prev = even & (seq >= 2)
    partners.append((to_core, in_seq(seq + 1)))
    partners.append((to_next, in_seq(seq + 2)))
    partners.append((~even, in_seq(seq - 1)))
    partners.append((from_prev, in_seq(seq - 2)))
    for h, c in spare:
        partners.append((first & (head == h), in_first(c)))
        partners.append((first & (head == c), in_first(h)))

    barrier = pltpu.get_barrier_semaphore()
    expected = jnp.int32(0)
    for holds, where in partners:
        @pl.when(holds)
        def _(where=where):
            pl.semaphore_signal(barrier, inc=1, device_id=where, device_id_type=MESH)
        expected = expected + holds.astype(jnp.int32)

    for g in range(G):
        own[g, 0] = k_ref[:, g * D:(g + 1) * D]
        own[g, 1] = v_ref[:, g * D:(g + 1) * D]
    for d in range(1, BACK + 1):
        @pl.when(b < d)
        def _(d=d):
            for g in range(G):
                window[g, d - 1] = jnp.zeros((2, T, D), jnp.bfloat16)

    pl.semaphore_wait(barrier, expected)

    def w_copy(g, d):
        return remote(own.at[g], window.at[g, d - 1], w_send.at[g, d - 1], w_recv.at[g, d - 1], device(b + d))

    def s_copy(g, step):
        return remote(sunk.at[g], sunk.at[g], s_send.at[g, step - 1], s_recv.at[g], in_seq(seq + step))

    def x_copy(g, h, c):
        return remote(own.at[g], sunk.at[g, c], x_send.at[g, h], x_recv.at[g, c], in_first(h))

    def g_copy(g, d):
        return remote(gsend.at[g, d - 1], grecv.at[g, d - 1], g_send.at[g, d - 1], g_recv.at[g, d - 1], device(b - d))

    def r_copy(g, step):
        return remote(rsend.at[g], rrecv.at[g, step - 1], r_send.at[g], r_recv.at[g, step - 1], in_seq(seq - step))

    def y_copy(g, h, c):
        return remote(rsend.at[g, c], yrecv.at[h, g], y_send.at[g, c], y_recv.at[h, g], in_first(c))

    def start_sends(g, carry):
        for d in range(1, BACK + 1):
            @pl.when(b + d < total)
            def _(d=d):
                w_copy(g, d).start()
        for h, c in spare:
            @pl.when(first & (head == c))
            def _(h=h, c=c):
                x_copy(g, h, c).start()
        return carry

    lax.fori_loop(0, G, start_sends, 0)

    def wait_window(g):
        for d in range(1, BACK + 1):
            @pl.when(b >= d)
            def _(d=d):
                w_copy(g, d).wait_recv()

    def arrive(g):
        @pl.when(first)
        def _():
            wait_window(g)
            for c in range(SMAX):
                @pl.when(head == c)
                def _(c=c):
                    sunk[g, c] = own[g]
                for d in range(1, BACK + 1):
                    @pl.when(head == c + d)
                    def _(c=c, d=d):
                        sunk[g, c] = window[g, d - 1]
            for h, c in spare:
                @pl.when(head == h)
                def _(h=h, c=c):
                    x_copy(g, h, c).wait_recv()

        @pl.when(seq > 0)
        def _():
            s_copy(g, 1).wait_recv()

        @pl.when(to_next)
        def _():
            s_copy(g, 2).start()

        @pl.when(to_core)
        def _():
            s_copy(g, 1).start()

    key_row = lax.broadcasted_iota(jnp.int32, (T, GROUP * T), 0)
    query_col = lax.rem(lax.broadcasted_iota(jnp.int32, (T, GROUP * T), 1), T)

    def compute(g):
        @pl.when(seq > 0)
        def _():
            wait_window(g)

        def stacked(kind):
            return jnp.concatenate(
                [own[g, kind]] + [window[g, d, kind] for d in range(BACK)]
                + [sunk[g, c, kind] for c in range(SMAX)], 0)

        def columns(r):
            return pl.ds(pl.multiple_of((g * GROUP + r) * D, D), D)

        k_all = stacked(0)
        v_all = stacked(1)
        q_all = jnp.concatenate([q_ref[:, columns(r)] for r in range(GROUP)], 0)
        go_all = jnp.concatenate([go_ref[:, columns(r)] for r in range(GROUP)], 0)
        wide = jnp.concatenate([jnp.full((1, T), win_ref[g * GROUP + r], jnp.int32) for r in range(GROUP)], 1)
        depth = jnp.concatenate([jnp.full((1, T), sink_ref[g * GROUP + r], jnp.int32) for r in range(GROUP)], 1)
        contract = (((1,), (1,)), ((), ()))
        raw = lax.dot_general(k_all, q_all, contract, preferred_element_type=jnp.float32)
        grad_w = lax.dot_general(v_all, go_all, contract, preferred_element_type=jnp.float32)
        raw = raw * (scale * math.log2(math.e))
        slots = [jnp.where(key_row <= query_col, raw[:T], NEG_FILL)]
        for d in range(1, WMAX):
            ok = (wide > d) & (b >= d)
            slots.append(raw[d * T:(d + 1) * T] + jnp.where(ok, 0.0, NEG_FILL))
        for c in range(SMAX):
            ok = (depth > c) & (wide <= b - c)
            slots.append(raw[(WMAX + c) * T:(WMAX + c + 1) * T] + jnp.where(ok, 0.0, NEG_FILL))
        scores = jnp.concatenate(slots, 0)
        top = jnp.max(scores, 0, keepdims=True)
        e = jnp.exp2(scores - top)
        inv = 1.0 / jnp.sum(e, 0, keepdims=True)
        weights = e * inv
        row_dot = jnp.sum(weights * grad_w, 0, keepdims=True)
        weights_b = weights.astype(jnp.bfloat16)
        dscore_b = (weights * (grad_w - row_dot)).astype(jnp.bfloat16)
        dq_t = lax.dot_general(k_all, dscore_b, (((0,), (0,)), ((), ())), preferred_element_type=jnp.float32)
        dq_t = dq_t * scale
        for r in range(GROUP):
            dq_ref[:, columns(r)] = dq_t[:, r * T:(r + 1) * T].T.astype(jnp.bfloat16)
        natural = (((1,), (0,)), ((), ()))
        dk = lax.dot_general(dscore_b, q_all, natural, preferred_element_type=jnp.float32) * scale
        dv = lax.dot_general(weights_b, go_all, natural, preferred_element_type=jnp.float32)
        for c in range(SMAX):
            rows = slice((WMAX + c) * T, (WMAX + c + 1) * T)
            rpart[g, c, 0] = dk[rows]
            rpart[g, c, 1] = dv[rows]

        @pl.when(~even)
        def _():
            rsend[g] = rpart[g].astype(jnp.bfloat16)
            r_copy(g, 1).start()

        for d in range(1, WMAX):
            rows = slice(d * T, (d + 1) * T)
            gsend[g, d - 1, 0] = dk[rows].astype(jnp.bfloat16)
            gsend[g, d - 1, 1] = dv[rows].astype(jnp.bfloat16)
            later = first & (head >= d) & (head < d + SMAX)

            @pl.when((b >= d) & ~later)
            def _(d=d):
                g_copy(g, d).start()
        gown[g, 0] = dk[:T]
        gown[g, 1] = dv[:T]

    def reduce(g):
        @pl.when(to_core)
        def _():
            r_copy(g, 1).wait_recv()
            rpart[g] = rpart[g] + rrecv[g, 0].astype(jnp.float32)

        @pl.when(to_next)
        def _():
            r_copy(g, 2).wait_recv()
            rpart[g] = rpart[g] + rrecv[g, 1].astype(jnp.float32)

        @pl.when(from_prev)
        def _():
            rsend[g] = rpart[g].astype(jnp.bfloat16)
            r_copy(g, 2).start()

        @pl.when(first)
        def _():
            for c in range(SMAX):
                @pl.when(head == c)
                def _(c=c):
                    gown[g] = gown[g] + rpart[g, c]
                for d in range(1, BACK + 1):
                    @pl.when(head == c + d)
                    def _(c=c, d=d):
                        gsend[g, d - 1] = (gsend[g, d - 1].astype(jnp.float32) + rpart[g, c]).astype(jnp.bfloat16)
                        g_copy(g, d).start()
            for h, c in spare:
                @pl.when(head == h)
                def _(h=h, c=c):
                    rsend[g, c] = rpart[g, c].astype(jnp.bfloat16)
                    y_copy(g, h, c).start()

    lag = jnp.minimum(1 + 2 * lax.div(seq_count - 1 - seq, 2), G)

    def prologue(g, carry):
        arrive(g)
        return carry

    lax.fori_loop(0, LOOK, prologue, 0)

    def step(i, carry):
        @pl.when(i + LOOK < G)
        def _():
            arrive(i + LOOK)

        @pl.when(i < G)
        def _():
            compute(i)

        j = i - lag

        @pl.when(even & (j >= 0) & (j < G))
        def _():
            reduce(j)
        return carry

    lax.fori_loop(0, 2 * G, step, 0)

    def finish(g, carry):
        for d in range(1, BACK + 1):
            @pl.when(b + d < total)
            def _(d=d):
                g_copy(g, d).wait_recv()
                gown[g] = gown[g] + grecv[g, d - 1].astype(jnp.float32)
        for h, c in spare:
            @pl.when(first & (head == c))
            def _(h=h, c=c):
                y_copy(g, h, c).wait_recv()
                gown[g] = gown[g] + yrecv[h, g].astype(jnp.float32)
        cols = pl.ds(pl.multiple_of(g * D, D), D)
        dk_ref[:, cols] = gown[g, 0].astype(jnp.bfloat16)
        dv_ref[:, cols] = gown[g, 1].astype(jnp.bfloat16)
        return carry

    lax.fori_loop(0, G, finish, 0)

    def drain(g, carry):
        for d in range(1, BACK + 1):
            @pl.when(b + d < total)
            def _(d=d):
                w_copy(g, d).wait_send()

            @pl.when(b >= d)
            def _(d=d):
                g_copy(g, d).wait_send()

        @pl.when(to_next)
        def _():
            s_copy(g, 2).wait_send()

        @pl.when(to_core)
        def _():
            s_copy(g, 1).wait_send()

        @pl.when(~even)
        def _():
            r_copy(g, 1).wait_send()

        @pl.when(from_prev)
        def _():
            r_copy(g, 2).wait_send()

        for h, c in spare:
            @pl.when(first & (head == c))
            def _(h=h, c=c):
                x_copy(g, h, c).wait_send()

            @pl.when(first & (head == h))
            def _(h=h, c=c):
                y_copy(g, h, c).wait_send()
        return carry

    lax.fori_loop(0, G, drain, 0)


def shards(head_count, seq_count, queries, keys, values, output_gradient, windows, sinks):
    G, D, T = KEY_VALUE_HEADS, HEAD_DIMENSION, BLOCK_TOKENS
    assert queries.shape[1] == T
    bf16, f32 = jnp.bfloat16, jnp.float32
    dma = pltpu.SemaphoreType.DMA
    vmem = pl.BlockSpec(memory_space=pltpu.VMEM)
    smem = pl.BlockSpec(memory_space=pltpu.SMEM)
    dq, dk, dv = pl.pallas_call(
        functools.partial(kernel, head_count, seq_count),
        out_shape=(
            jax.ShapeDtypeStruct((T, QUERY_HEADS * D), bf16),
            jax.ShapeDtypeStruct((T, G * D), bf16),
            jax.ShapeDtypeStruct((T, G * D), bf16),
        ),
        in_specs=[vmem] * 4 + [smem] * 2,
        out_specs=(vmem,) * 3,
        scratch_shapes=[
            pltpu.VMEM((G, 2, T, D), bf16),
            pltpu.VMEM((G, BACK, 2, T, D), bf16),
            pltpu.VMEM((G, SMAX, 2, T, D), bf16),
            pltpu.VMEM((G, BACK, 2, T, D), bf16),
            pltpu.VMEM((G, BACK, 2, T, D), bf16),
            pltpu.VMEM((G, SMAX, 2, T, D), bf16),
            pltpu.VMEM((G, 2, SMAX, 2, T, D), bf16),
            pltpu.VMEM((G, 2, T, D), f32),
            pltpu.VMEM((G, SMAX, 2, T, D), f32),
            pltpu.VMEM((head_count, G, 2, T, D), bf16),
            dma((G, BACK)), dma((G, BACK)),
            dma((G, 2)), dma((G,)),
            dma((G, head_count)), dma((G, SMAX)),
            dma((G, BACK)), dma((G, BACK)),
            dma((G,)), dma((G, 2)),
            dma((G, SMAX)), dma((head_count, G)),
        ],
        compiler_params=pltpu.CompilerParams(
            collective_id=0, has_side_effects=True, vmem_limit_bytes=52 * 2**20),
    )(queries[0], keys[0], values[0], output_gradient[0], windows, sinks)
    return dq[None], dk[None], dv[None]


def solution(mesh):
    return jax.shard_map(
        functools.partial(shards, mesh.shape["head"], mesh.shape["seq"]),
        mesh=mesh,
        in_specs=(
            P("seq", "head", None),
            P("seq", "head", None),
            P("seq", "head", None),
            P("seq", "head", None),
            P(),
            P(),
        ),
        out_specs=(P("seq", "head", None), P("seq", "head", None), P("seq", "head", None)),
        check_vma=False,
    )
```

```python
import functools
import math

import jax
import jax.numpy as jnp
from jax import lax
from jax.experimental import pallas as pl
from jax.experimental.pallas import tpu as pltpu
from jax.sharding import PartitionSpec as P

QUERY_HEADS = 32
KEY_VALUE_HEADS = 8
HEAD_DIMENSION = 128
BLOCK_TOKENS = 128
WMAX = 4
SMAX = 2

NEG_FILL = -1e30
GROUP = QUERY_HEADS // KEY_VALUE_HEADS
BACK = WMAX - 1
LOOK = 2
HOLD = 2
PAIRS = ((1, 3, 0, 0), (2, 3, 0, 1), (2, 1, 1, 0), (3, 1, 1, 1))
MESH = pl.DeviceIdType.MESH


def spare_links(head_count):
    return [
        (h, c)
        for c in range(SMAX)
        for h in range(head_count)
        if h != c and not 1 <= h - c <= BACK
    ]


def kernel(
    head_count,
    seq_count,
    q_hbm, k_hbm, v_hbm, go_hbm, win_ref, sink_ref,
    dq_ref, dk_ref, dv_ref,
    q_ref, go_ref, prel, own, window, sunk, gsend, grecv, rsend, rrecv, gown, rpart, yrecv,
    w_send, w_recv, s_send, s_recv, x_send, x_recv,
    g_send, g_recv, r_send, r_recv, y_send, y_recv,
    f_send, p_send, p_recv, in_sem,
):
    G = KEY_VALUE_HEADS
    D = HEAD_DIMENSION
    T = BLOCK_TOKENS
    head = lax.axis_index("head")
    seq = lax.axis_index("seq")
    total = head_count * seq_count
    b = seq * head_count + head
    even = lax.rem(seq, 2) == 0
    first = seq == 0
    scale = 1.0 / math.sqrt(D)
    spare = spare_links(head_count)

    def device(block):
        return {"head": lax.rem(block + total, total) % head_count,
                "seq": lax.div(lax.rem(block + total, total), head_count)}

    def in_seq(s):
        return {"head": head, "seq": lax.rem(s + 2 * seq_count, seq_count)}

    def in_first(h):
        return {"head": h, "seq": 0}

    def remote(src, dst, ssem, rsem, where):
        return pltpu.make_async_remote_copy(
            src_ref=src, dst_ref=dst, send_sem=ssem, recv_sem=rsem,
            device_id=where, device_id_type=MESH)

    partners = []
    for d in range(1, BACK + 1):
        partners.append((b + d < total, device(b + d)))
        partners.append((b >= d, device(b - d)))
    to_core = even & (seq + 1 < seq_count)
    to_next = even & (seq + 2 < seq_count)
    from_prev = even & (seq >= 2)
    partners.append((to_core, in_seq(seq + 1)))
    partners.append((to_next, in_seq(seq + 2)))
    partners.append((~even, in_seq(seq - 1)))
    partners.append((from_prev, in_seq(seq - 2)))
    for h, c in spare:
        partners.append((first & (head == h), in_first(c)))
        partners.append((first & (head == c), in_first(h)))

    def in_copies(g):
        cols = pl.ds(pl.multiple_of(g * D, D), D)
        wide_cols = pl.ds(pl.multiple_of(g * GROUP * D, GROUP * D), GROUP * D)
        return (
            pltpu.make_async_copy(k_hbm.at[:, cols], own.at[g, 0], in_sem.at[g, 0]),
            pltpu.make_async_copy(v_hbm.at[:, cols], own.at[g, 1], in_sem.at[g, 1]),
            pltpu.make_async_copy(q_hbm.at[:, wide_cols], q_ref.at[:, wide_cols], in_sem.at[g, 2]),
            pltpu.make_async_copy(go_hbm.at[:, wide_cols], go_ref.at[:, wide_cols], in_sem.at[g, 3]),
        )

    def relayed(block, g, pair):
        near, far, parity, turn = pair
        if head_count != 4:
            return jnp.bool_(False)
        return ((block >= 0) & (lax.rem(block + total, 2) == parity) & (lax.rem(g, 2) == turn)
                & (block + max(near, far) < total))

    def relayed_to(block, g, d):
        hit = jnp.bool_(False)
        for pair in PAIRS:
            if pair[1] == d:
                hit = hit | relayed(block, g, pair)
        return hit

    def load_kv(g, carry):
        for copy in in_copies(g)[:2]:
            copy.start()
        return carry

    def load_q(g, carry):
        for copy in in_copies(g)[2:]:
            copy.start()
        return carry

    lax.fori_loop(0, G, load_kv, 0)
    lax.fori_loop(0, G, load_q, 0)

    barrier = pltpu.get_barrier_semaphore()
    expected = jnp.int32(0)
    for holds, where in partners:
        @pl.when(holds)
        def _(where=where):
            pl.semaphore_signal(barrier, inc=1, device_id=where, device_id_type=MESH)
        expected = expected + holds.astype(jnp.int32)

    for d in range(1, BACK + 1):
        @pl.when(b < d)
        def _(d=d):
            for g in range(G):
                window[g, d - 1] = jnp.zeros((2, T, D), jnp.bfloat16)

    pl.semaphore_wait(barrier, expected)

    def w_copy(g, d):
        return remote(own.at[g], window.at[g, d - 1], w_send.at[g, d - 1], w_recv.at[g, d - 1], device(b + d))

    def s_copy(g, step):
        return remote(sunk.at[g], sunk.at[g], s_send.at[g, step - 1], s_recv.at[g], in_seq(seq + step))

    def x_copy(g, h, c):
        return remote(own.at[g], sunk.at[g, c], x_send.at[g, h], x_recv.at[g, c], in_first(h))

    def g_copy(g, d):
        return remote(gsend.at[g, d - 1], grecv.at[g, d - 1], g_send.at[g, d - 1], g_recv.at[g, d - 1], device(b - d))

    def r_copy(g, step):
        return remote(rsend.at[g], rrecv.at[g, step - 1], r_send.at[g], r_recv.at[g, step - 1], in_seq(seq - step))

    def y_copy(g, h, c):
        return remote(rsend.at[g, c], yrecv.at[h, g], y_send.at[g, c], y_recv.at[h, g], in_first(c))

    def f_copy(g, near, far):
        return remote(window.at[g, near - 1], window.at[g, far - 1], f_send.at[g], w_recv.at[g, far - 1],
                      device(b + far - near))

    def p_copy(g, near, far):
        return remote(gsend.at[g, far - 1], prel.at[g, near - 1], p_send.at[g], p_recv.at[g, near - 1],
                      device(b - far + near))

    def start_sends(g, carry):
        for copy in in_copies(g)[:2]:
            copy.wait()
        for d in range(1, BACK + 1):
            @pl.when((b + d < total) & ~relayed_to(b, g, d))
            def _(d=d):
                w_copy(g, d).start()
        for h, c in spare:
            @pl.when(first & (head == c))
            def _(h=h, c=c):
                x_copy(g, h, c).start()
        return carry

    lax.fori_loop(0, G, start_sends, 0)

    def passes(g, d):
        hit = jnp.bool_(False)
        for pair in PAIRS:
            if pair[0] == d:
                hit = hit | relayed(b - d, g, pair)
        return hit

    def wait_window(g):
        for d in range(1, BACK + 1):
            @pl.when((b >= d) & ~passes(g, d))
            def _(d=d):
                w_copy(g, d).wait_recv()

    def arrive(g):
        for pair in PAIRS:
            @pl.when(relayed(b - pair[0], g, pair))
            def _(near=pair[0], far=pair[1]):
                w_copy(g, near).wait_recv()
                f_copy(g, near, far).start()

        @pl.when(first)
        def _():
            wait_window(g)
            for c in range(SMAX):
                @pl.when(head == c)
                def _(c=c):
                    sunk[g, c] = own[g]
                for d in range(1, BACK + 1):
                    @pl.when(head == c + d)
                    def _(c=c, d=d):
                        sunk[g, c] = window[g, d - 1]
            for h, c in spare:
                @pl.when(head == h)
                def _(h=h, c=c):
                    x_copy(g, h, c).wait_recv()

        @pl.when(seq > 0)
        def _():
            s_copy(g, 1).wait_recv()

        @pl.when(to_next)
        def _():
            s_copy(g, 2).start()

        @pl.when(to_core)
        def _():
            s_copy(g, 1).start()

    key_row = lax.broadcasted_iota(jnp.int32, (T, GROUP * T), 0)
    query_col = lax.rem(lax.broadcasted_iota(jnp.int32, (T, GROUP * T), 1), T)

    def compute(g):
        @pl.when(seq > 0)
        def _():
            wait_window(g)

        for copy in in_copies(g)[2:]:
            copy.wait()

        def stacked(kind):
            return jnp.concatenate(
                [own[g, kind]] + [window[g, d, kind] for d in range(BACK)]
                + [sunk[g, c, kind] for c in range(SMAX)], 0)

        def columns(r):
            return pl.ds(pl.multiple_of((g * GROUP + r) * D, D), D)

        k_all = stacked(0)
        v_all = stacked(1)
        q_all = jnp.concatenate([q_ref[:, columns(r)] for r in range(GROUP)], 0)
        go_all = jnp.concatenate([go_ref[:, columns(r)] for r in range(GROUP)], 0)
        wide = jnp.concatenate([jnp.full((1, T), win_ref[g * GROUP + r], jnp.int32) for r in range(GROUP)], 1)
        depth = jnp.concatenate([jnp.full((1, T), sink_ref[g * GROUP + r], jnp.int32) for r in range(GROUP)], 1)
        contract = (((1,), (1,)), ((), ()))
        raw = lax.dot_general(k_all, q_all, contract, preferred_element_type=jnp.float32)
        grad_w = lax.dot_general(v_all, go_all, contract, preferred_element_type=jnp.float32)
        raw = raw * (scale * math.log2(math.e))
        slots = [jnp.where(key_row <= query_col, raw[:T], NEG_FILL)]
        for d in range(1, WMAX):
            ok = (wide > d) & (b >= d)
            slots.append(raw[d * T:(d + 1) * T] + jnp.where(ok, 0.0, NEG_FILL))
        for c in range(SMAX):
            ok = (depth > c) & (wide <= b - c)
            slots.append(raw[(WMAX + c) * T:(WMAX + c + 1) * T] + jnp.where(ok, 0.0, NEG_FILL))
        scores = jnp.concatenate(slots, 0)
        top = jnp.max(scores, 0, keepdims=True)
        e = jnp.exp2(scores - top)
        inv = 1.0 / jnp.sum(e, 0, keepdims=True)
        weights = e * inv
        row_dot = jnp.sum(weights * grad_w, 0, keepdims=True)
        weights_b = weights.astype(jnp.bfloat16)
        dscore_b = (weights * (grad_w - row_dot)).astype(jnp.bfloat16)
        dq_t = lax.dot_general(k_all, dscore_b, (((0,), (0,)), ((), ())), preferred_element_type=jnp.float32)
        dq_t = dq_t * scale
        for r in range(GROUP):
            dq_ref[:, columns(r)] = dq_t[:, r * T:(r + 1) * T].T.astype(jnp.bfloat16)
        natural = (((1,), (0,)), ((), ()))
        dk = lax.dot_general(dscore_b, q_all, natural, preferred_element_type=jnp.float32) * scale
        dv = lax.dot_general(weights_b, go_all, natural, preferred_element_type=jnp.float32)
        for c in range(SMAX):
            rows = slice((WMAX + c) * T, (WMAX + c + 1) * T)
            rpart[g, c, 0] = dk[rows]
            rpart[g, c, 1] = dv[rows]

        @pl.when(~even)
        def _():
            rsend[g] = rpart[g].astype(jnp.bfloat16)
            r_copy(g, 1).start()

        for d in range(1, WMAX):
            rows = slice(d * T, (d + 1) * T)
            gsend[g, d - 1, 0] = dk[rows].astype(jnp.bfloat16)
            gsend[g, d - 1, 1] = dv[rows].astype(jnp.bfloat16)
            later = first & (head >= d) & (head < d + SMAX)
            direct = (b >= d) & ~later
            kept = b - d >= SMAX

            @pl.when(direct & ~(kept & (relayed_to(b - d, g, d) | passes(g, d))))
            def _(d=d):
                g_copy(g, d).start()

            for pair in PAIRS:
                if pair[1] == d:
                    @pl.when(kept & relayed(b - d, g, pair))
                    def _(near=pair[0], far=pair[1]):
                        p_copy(g, near, far).start()
        gown[g, 0] = dk[:T]
        gown[g, 1] = dv[:T]

    def reduce(g):
        @pl.when(to_core)
        def _():
            r_copy(g, 1).wait_recv()
            rpart[g] = rpart[g] + rrecv[g, 0].astype(jnp.float32)

        @pl.when(to_next)
        def _():
            r_copy(g, 2).wait_recv()
            rpart[g] = rpart[g] + rrecv[g, 1].astype(jnp.float32)

        @pl.when(from_prev)
        def _():
            rsend[g] = rpart[g].astype(jnp.bfloat16)
            r_copy(g, 2).start()

        @pl.when(first)
        def _():
            for c in range(SMAX):
                @pl.when(head == c)
                def _(c=c):
                    gown[g] = gown[g] + rpart[g, c]
                for d in range(1, BACK + 1):
                    @pl.when(head == c + d)
                    def _(c=c, d=d):
                        gsend[g, d - 1] = (gsend[g, d - 1].astype(jnp.float32) + rpart[g, c]).astype(jnp.bfloat16)
                        g_copy(g, d).start()
            for h, c in spare:
                @pl.when(head == h)
                def _(h=h, c=c):
                    rsend[g, c] = rpart[g, c].astype(jnp.bfloat16)
                    y_copy(g, h, c).start()

    def merge(g):
        for d in range(1, BACK + 1):
            @pl.when((b - d >= SMAX) & passes(g, d))
            def _(d=d):
                p_copy(g, d, d).wait_recv()
                gsend[g, d - 1] = (
                    gsend[g, d - 1].astype(jnp.float32) + prel[g, d - 1].astype(jnp.float32)
                ).astype(jnp.bfloat16)
                g_copy(g, d).start()

    lag = jnp.minimum(1 + 2 * lax.div(seq_count - 1 - seq, 2), G)

    def prologue(g, carry):
        arrive(g)
        return carry

    lax.fori_loop(0, LOOK, prologue, 0)

    def step(i, carry):
        @pl.when(i + LOOK < G)
        def _():
            arrive(i + LOOK)

        @pl.when(i < G)
        def _():
            compute(i)

        @pl.when((i >= HOLD) & (i - HOLD < G))
        def _():
            merge(i - HOLD)

        j = i - lag

        @pl.when(even & (j >= 0) & (j < G))
        def _():
            reduce(j)
        return carry

    lax.fori_loop(0, 2 * G, step, 0)

    def finish(g, carry):
        for d in range(1, BACK + 1):
            @pl.when((b + d < total) & ~((b >= SMAX) & relayed_to(b, g, d)))
            def _(d=d):
                g_copy(g, d).wait_recv()
                gown[g] = gown[g] + grecv[g, d - 1].astype(jnp.float32)
        for h, c in spare:
            @pl.when(first & (head == c))
            def _(h=h, c=c):
                y_copy(g, h, c).wait_recv()
                gown[g] = gown[g] + yrecv[h, g].astype(jnp.float32)
        cols = pl.ds(pl.multiple_of(g * D, D), D)
        dk_ref[:, cols] = gown[g, 0].astype(jnp.bfloat16)
        dv_ref[:, cols] = gown[g, 1].astype(jnp.bfloat16)
        return carry

    lax.fori_loop(0, G, finish, 0)

    def drain(g, carry):
        for d in range(1, BACK + 1):
            @pl.when((b + d < total) & ~relayed_to(b, g, d))
            def _(d=d):
                w_copy(g, d).wait_send()

            @pl.when((b >= d) & ~((b - d >= SMAX) & relayed_to(b - d, g, d)))
            def _(d=d):
                g_copy(g, d).wait_send()

        for pair in PAIRS:
            @pl.when(relayed(b - pair[0], g, pair))
            def _(near=pair[0], far=pair[1]):
                f_copy(g, near, far).wait_send()

            @pl.when((b - pair[1] >= SMAX) & relayed(b - pair[1], g, pair))
            def _(near=pair[0], far=pair[1]):
                p_copy(g, near, far).wait_send()

        @pl.when(to_next)
        def _():
            s_copy(g, 2).wait_send()

        @pl.when(to_core)
        def _():
            s_copy(g, 1).wait_send()

        @pl.when(~even)
        def _():
            r_copy(g, 1).wait_send()

        @pl.when(from_prev)
        def _():
            r_copy(g, 2).wait_send()

        for h, c in spare:
            @pl.when(first & (head == c))
            def _(h=h, c=c):
                x_copy(g, h, c).wait_send()

            @pl.when(first & (head == h))
            def _(h=h, c=c):
                y_copy(g, h, c).wait_send()
        return carry

    lax.fori_loop(0, G, drain, 0)


def shards(head_count, seq_count, queries, keys, values, output_gradient, windows, sinks):
    G, D, T = KEY_VALUE_HEADS, HEAD_DIMENSION, BLOCK_TOKENS
    assert queries.shape[1] == T
    bf16, f32 = jnp.bfloat16, jnp.float32
    dma = pltpu.SemaphoreType.DMA
    vmem = pl.BlockSpec(memory_space=pltpu.VMEM)
    smem = pl.BlockSpec(memory_space=pltpu.SMEM)
    dq, dk, dv = pl.pallas_call(
        functools.partial(kernel, head_count, seq_count),
        out_shape=(
            jax.ShapeDtypeStruct((T, QUERY_HEADS * D), bf16),
            jax.ShapeDtypeStruct((T, G * D), bf16),
            jax.ShapeDtypeStruct((T, G * D), bf16),
        ),
        in_specs=[pl.BlockSpec(memory_space=pltpu.HBM)] * 4 + [smem] * 2,
        out_specs=(vmem,) * 3,
        scratch_shapes=[
            pltpu.VMEM((T, QUERY_HEADS * D), bf16),
            pltpu.VMEM((T, QUERY_HEADS * D), bf16),
            pltpu.VMEM((G, BACK, 2, T, D), bf16),
            pltpu.VMEM((G, 2, T, D), bf16),
            pltpu.VMEM((G, BACK, 2, T, D), bf16),
            pltpu.VMEM((G, SMAX, 2, T, D), bf16),
            pltpu.VMEM((G, BACK, 2, T, D), bf16),
            pltpu.VMEM((G, BACK, 2, T, D), bf16),
            pltpu.VMEM((G, SMAX, 2, T, D), bf16),
            pltpu.VMEM((G, 2, SMAX, 2, T, D), bf16),
            pltpu.VMEM((G, 2, T, D), f32),
            pltpu.VMEM((G, SMAX, 2, T, D), f32),
            pltpu.VMEM((head_count, G, 2, T, D), bf16),
            dma((G, BACK)), dma((G, BACK)),
            dma((G, 2)), dma((G,)),
            dma((G, head_count)), dma((G, SMAX)),
            dma((G, BACK)), dma((G, BACK)),
            dma((G,)), dma((G, 2)),
            dma((G, SMAX)), dma((head_count, G)),
            dma((G,)), dma((G,)), dma((G, BACK)), dma((G, 4)),
        ],
        compiler_params=pltpu.CompilerParams(
            collective_id=0, has_side_effects=True, vmem_limit_bytes=40 * 2**20),
    )(queries[0], keys[0], values[0], output_gradient[0], windows, sinks)
    return dq[None], dk[None], dv[None]


def solution(mesh):
    return jax.shard_map(
        functools.partial(shards, mesh.shape["head"], mesh.shape["seq"]),
        mesh=mesh,
        in_specs=(
            P("seq", "head", None),
            P("seq", "head", None),
            P("seq", "head", None),
            P("seq", "head", None),
            P(),
            P(),
        ),
        out_specs=(P("seq", "head", None), P("seq", "head", None), P("seq", "head", None)),
        check_vma=False,
    )
```

```python
import functools
import math

import jax
import jax.numpy as jnp
from jax import lax
from jax.experimental import pallas as pl
from jax.experimental.pallas import tpu as pltpu
from jax.sharding import PartitionSpec as P

QUERY_HEADS = 32
KEY_VALUE_HEADS = 8
HEAD_DIMENSION = 128
BLOCK_TOKENS = 128
WMAX = 4
SMAX = 2

NEG_FILL = -1e30
GROUP = QUERY_HEADS // KEY_VALUE_HEADS
BACK = WMAX - 1
LOOK = 2
AHEAD = 4
MESH = pl.DeviceIdType.MESH


def spare_links(head_count):
    return [
        (h, c)
        for c in range(SMAX)
        for h in range(head_count)
        if h != c and not 1 <= h - c <= BACK
    ]


def kernel(
    head_count,
    seq_count,
    q_hbm, k_hbm, v_hbm, go_hbm, win_ref, sink_ref,
    dq_ref, dk_ref, dv_ref,
    q_ref, go_ref, sc, gw, wb, ds, own, window, sunk, gsend, grecv, rsend, rrecv, gown, rpart, yrecv,
    w_send, w_recv, s_send, s_recv, x_send, x_recv,
    g_send, g_recv, r_send, r_recv, y_send, y_recv, in_sem,
):
    G = KEY_VALUE_HEADS
    D = HEAD_DIMENSION
    T = BLOCK_TOKENS
    head = lax.axis_index("head")
    seq = lax.axis_index("seq")
    total = head_count * seq_count
    b = seq * head_count + head
    even = lax.rem(seq, 2) == 0
    first = seq == 0
    scale = 1.0 / math.sqrt(D)
    spare = spare_links(head_count)

    def device(block):
        return {"head": lax.rem(block + total, total) % head_count,
                "seq": lax.div(lax.rem(block + total, total), head_count)}

    def in_seq(s):
        return {"head": head, "seq": lax.rem(s + 2 * seq_count, seq_count)}

    def in_first(h):
        return {"head": h, "seq": 0}

    def remote(src, dst, ssem, rsem, where):
        return pltpu.make_async_remote_copy(
            src_ref=src, dst_ref=dst, send_sem=ssem, recv_sem=rsem,
            device_id=where, device_id_type=MESH)

    partners = []
    for d in range(1, BACK + 1):
        partners.append((b + d < total, device(b + d)))
        partners.append((b >= d, device(b - d)))
    to_core = even & (seq + 1 < seq_count)
    to_next = even & (seq + 2 < seq_count)
    from_prev = even & (seq >= 2)
    partners.append((to_core, in_seq(seq + 1)))
    partners.append((to_next, in_seq(seq + 2)))
    partners.append((~even, in_seq(seq - 1)))
    partners.append((from_prev, in_seq(seq - 2)))
    for h, c in spare:
        partners.append((first & (head == h), in_first(c)))
        partners.append((first & (head == c), in_first(h)))

    def kv_copies(g):
        cols = pl.ds(pl.multiple_of(g * D, D), D)
        return (pltpu.make_async_copy(k_hbm.at[:, cols], own.at[g, 0], in_sem.at[g, 0]),
                pltpu.make_async_copy(v_hbm.at[:, cols], own.at[g, 1], in_sem.at[g, 1]))

    def q_copies(g):
        cols = pl.ds(pl.multiple_of(g * GROUP * D, GROUP * D), GROUP * D)
        return (pltpu.make_async_copy(q_hbm.at[:, cols], q_ref.at[:, cols], in_sem.at[g, 2]),
                pltpu.make_async_copy(go_hbm.at[:, cols], go_ref.at[:, cols], in_sem.at[g, 3]))

    def load_kv(g, carry):
        for copy in kv_copies(g):
            copy.start()
        return carry

    def load_q(g, carry):
        for copy in q_copies(g):
            copy.start()
        return carry

    lax.fori_loop(0, G, load_kv, 0)
    lax.fori_loop(0, G, load_q, 0)

    barrier = pltpu.get_barrier_semaphore()
    expected = jnp.int32(0)
    for holds, where in partners:
        @pl.when(holds)
        def _(where=where):
            pl.semaphore_signal(barrier, inc=1, device_id=where, device_id_type=MESH)
        expected = expected + holds.astype(jnp.int32)

    for d in range(1, BACK + 1):
        @pl.when(b < d)
        def _(d=d):
            for g in range(G):
                window[g, d - 1] = jnp.zeros((2, T, D), jnp.bfloat16)

    pl.semaphore_wait(barrier, expected)

    def w_copy(g, d):
        return remote(own.at[g], window.at[g, d - 1], w_send.at[g, d - 1], w_recv.at[g, d - 1], device(b + d))

    def s_copy(g, step):
        return remote(sunk.at[g], sunk.at[g], s_send.at[g, step - 1], s_recv.at[g], in_seq(seq + step))

    def x_copy(g, h, c):
        return remote(own.at[g], sunk.at[g, c], x_send.at[g, h], x_recv.at[g, c], in_first(h))

    def g_copy(g, d):
        return remote(gsend.at[g, d - 1], grecv.at[g, d - 1], g_send.at[g, d - 1], g_recv.at[g, d - 1], device(b - d))

    def r_copy(g, step):
        return remote(rsend.at[g], rrecv.at[g, step - 1], r_send.at[g], r_recv.at[g, step - 1], in_seq(seq - step))

    def y_copy(g, h, c):
        return remote(rsend.at[g, c], yrecv.at[h, g], y_send.at[g, c], y_recv.at[h, g], in_first(c))

    def start_sends(g, carry):
        for copy in kv_copies(g):
            copy.wait()
        for d in range(1, BACK + 1):
            @pl.when(b + d < total)
            def _(d=d):
                w_copy(g, d).start()
        for h, c in spare:
            @pl.when(first & (head == c))
            def _(h=h, c=c):
                x_copy(g, h, c).start()
        return carry

    lax.fori_loop(0, AHEAD, start_sends, 0)

    def wait_window(g):
        for d in range(1, BACK + 1):
            @pl.when(b >= d)
            def _(d=d):
                w_copy(g, d).wait_recv()

    def arrive(g):
        @pl.when(first)
        def _():
            wait_window(g)
            for c in range(SMAX):
                @pl.when(head == c)
                def _(c=c):
                    sunk[g, c] = own[g]
                for d in range(1, BACK + 1):
                    @pl.when(head == c + d)
                    def _(c=c, d=d):
                        sunk[g, c] = window[g, d - 1]
            for h, c in spare:
                @pl.when(head == h)
                def _(h=h, c=c):
                    x_copy(g, h, c).wait_recv()

        @pl.when(seq > 0)
        def _():
            s_copy(g, 1).wait_recv()

        @pl.when(to_next)
        def _():
            s_copy(g, 2).start()

        @pl.when(to_core)
        def _():
            s_copy(g, 1).start()

    causal = lax.broadcasted_iota(jnp.int32, (T, T), 0) <= lax.broadcasted_iota(jnp.int32, (T, T), 1)

    def compute(g):
        @pl.when(seq > 0)
        def _():
            wait_window(g)

        for copy in q_copies(g):
            copy.wait()

        def stacked(kind):
            return jnp.concatenate(
                [own[g, kind]] + [window[g, d, kind] for d in range(BACK)]
                + [sunk[g, c, kind] for c in range(SMAX)], 0)

        def columns(r):
            return pl.ds(pl.multiple_of((g * GROUP + r) * D, D), D)

        k_all = stacked(0)
        v_all = stacked(1)
        q_all = jnp.concatenate([q_ref[:, columns(r)] for r in range(GROUP)], 0)
        go_all = jnp.concatenate([go_ref[:, columns(r)] for r in range(GROUP)], 0)
        wide = jnp.concatenate([jnp.full((1, T), win_ref[g * GROUP + r], jnp.int32) for r in range(GROUP)], 1)
        depth = jnp.concatenate([jnp.full((1, T), sink_ref[g * GROUP + r], jnp.int32) for r in range(GROUP)], 1)
        contract = (((1,), (1,)), ((), ()))
        for part in range(2):
            lanes = slice(part * 2 * T, (part + 1) * 2 * T)
            sc[:, lanes] = lax.dot_general(
                k_all, q_all[lanes], contract, preferred_element_type=jnp.float32)
            gw[:, lanes] = lax.dot_general(
                v_all, go_all[lanes], contract, preferred_element_type=jnp.float32)
        slots = WMAX + SMAX
        k_turned = k_all.astype(jnp.float32).T.astype(jnp.bfloat16)
        for r in range(GROUP):
            lanes = slice(r * T, (r + 1) * T)
            bias = [None]
            for d in range(1, WMAX):
                bias.append(jnp.where((wide[:, lanes] > d) & (b >= d), 0.0, NEG_FILL))
            for c in range(SMAX):
                bias.append(jnp.where((depth[:, lanes] > c) & (wide[:, lanes] <= b - c), 0.0, NEG_FILL))
            top = None
            for n in range(slots):
                rows = slice(n * T, (n + 1) * T)
                tile = sc[rows, lanes] * (scale * math.log2(math.e))
                if n == 0:
                    tile = jnp.where(causal, tile, NEG_FILL)
                else:
                    tile = tile + bias[n]
                sc[rows, lanes] = tile
                high = jnp.max(tile.reshape(T // 8, 8, T), 0)
                top = high if top is None else jnp.maximum(top, high)
            top = jnp.max(top, 0, keepdims=True)
            mass = dot = None
            for n in range(slots):
                rows = slice(n * T, (n + 1) * T)
                e = jnp.exp2(sc[rows, lanes] - top)
                sc[rows, lanes] = e
                mass_n = jnp.sum(e.reshape(T // 8, 8, T), 0)
                dot_n = jnp.sum((e * gw[rows, lanes]).reshape(T // 8, 8, T), 0)
                mass = mass_n if mass is None else mass + mass_n
                dot = dot_n if dot is None else dot + dot_n
            inv = 1.0 / jnp.sum(mass, 0, keepdims=True)
            row_dot = jnp.sum(dot, 0, keepdims=True) * inv
            for n in range(slots):
                rows = slice(n * T, (n + 1) * T)
                weights = sc[rows, lanes] * inv
                wb[rows, lanes] = weights.astype(jnp.bfloat16)
                ds[rows, lanes] = (weights * (gw[rows, lanes] - row_dot)).astype(jnp.bfloat16)
        weights_b = wb[...]
        dscore_b = ds[...]
        dq_t = lax.dot_general(k_turned, dscore_b, (((1,), (0,)), ((), ())), preferred_element_type=jnp.float32)
        dq_t = dq_t * scale
        for r in range(GROUP):
            dq_ref[:, columns(r)] = dq_t[:, r * T:(r + 1) * T].T.astype(jnp.bfloat16)
        natural = (((1,), (0,)), ((), ()))
        dk = lax.dot_general(dscore_b, q_all, natural, preferred_element_type=jnp.float32) * scale
        dv = lax.dot_general(weights_b, go_all, natural, preferred_element_type=jnp.float32)
        for c in range(SMAX):
            rows = slice((WMAX + c) * T, (WMAX + c + 1) * T)
            rpart[g, c, 0] = dk[rows]
            rpart[g, c, 1] = dv[rows]

        @pl.when(~even)
        def _():
            rsend[g] = rpart[g].astype(jnp.bfloat16)
            r_copy(g, 1).start()

        for d in range(1, WMAX):
            rows = slice(d * T, (d + 1) * T)
            gsend[g, d - 1, 0] = dk[rows].astype(jnp.bfloat16)
            gsend[g, d - 1, 1] = dv[rows].astype(jnp.bfloat16)
            later = first & (head >= d) & (head < d + SMAX)

            @pl.when((b >= d) & ~later)
            def _(d=d):
                g_copy(g, d).start()
        gown[g, 0] = dk[:T]
        gown[g, 1] = dv[:T]

    def reduce(g):
        @pl.when(to_core)
        def _():
            r_copy(g, 1).wait_recv()
            rpart[g] = rpart[g] + rrecv[g, 0].astype(jnp.float32)

        @pl.when(to_next)
        def _():
            r_copy(g, 2).wait_recv()
            rpart[g] = rpart[g] + rrecv[g, 1].astype(jnp.float32)

        @pl.when(from_prev)
        def _():
            rsend[g] = rpart[g].astype(jnp.bfloat16)
            r_copy(g, 2).start()

        @pl.when(first)
        def _():
            for c in range(SMAX):
                @pl.when(head == c)
                def _(c=c):
                    gown[g] = gown[g] + rpart[g, c]
                for d in range(1, BACK + 1):
                    @pl.when(head == c + d)
                    def _(c=c, d=d):
                        gsend[g, d - 1] = (gsend[g, d - 1].astype(jnp.float32) + rpart[g, c]).astype(jnp.bfloat16)
                        g_copy(g, d).start()
            for h, c in spare:
                @pl.when(head == h)
                def _(h=h, c=c):
                    rsend[g, c] = rpart[g, c].astype(jnp.bfloat16)
                    y_copy(g, h, c).start()

    lag = jnp.minimum(1 + 2 * lax.div(seq_count - 1 - seq, 2), G)

    def prologue(g, carry):
        arrive(g)
        return carry

    lax.fori_loop(0, LOOK, prologue, 0)

    def step(i, carry):
        @pl.when(i + AHEAD < G)
        def _():
            start_sends(i + AHEAD, 0)

        @pl.when(i + LOOK < G)
        def _():
            arrive(i + LOOK)

        @pl.when(i < G)
        def _():
            compute(i)

        j = i - lag

        @pl.when(even & (j >= 0) & (j < G))
        def _():
            reduce(j)
        return carry

    lax.fori_loop(0, 2 * G, step, 0)

    def finish(g, carry):
        for d in range(1, BACK + 1):
            @pl.when(b + d < total)
            def _(d=d):
                g_copy(g, d).wait_recv()
                gown[g] = gown[g] + grecv[g, d - 1].astype(jnp.float32)
        for h, c in spare:
            @pl.when(first & (head == c))
            def _(h=h, c=c):
                y_copy(g, h, c).wait_recv()
                gown[g] = gown[g] + yrecv[h, g].astype(jnp.float32)
        cols = pl.ds(pl.multiple_of(g * D, D), D)
        dk_ref[:, cols] = gown[g, 0].astype(jnp.bfloat16)
        dv_ref[:, cols] = gown[g, 1].astype(jnp.bfloat16)
        return carry

    lax.fori_loop(0, G, finish, 0)

    def drain(g, carry):
        for d in range(1, BACK + 1):
            @pl.when(b + d < total)
            def _(d=d):
                w_copy(g, d).wait_send()

            @pl.when(b >= d)
            def _(d=d):
                g_copy(g, d).wait_send()

        @pl.when(to_next)
        def _():
            s_copy(g, 2).wait_send()

        @pl.when(to_core)
        def _():
            s_copy(g, 1).wait_send()

        @pl.when(~even)
        def _():
            r_copy(g, 1).wait_send()

        @pl.when(from_prev)
        def _():
            r_copy(g, 2).wait_send()

        for h, c in spare:
            @pl.when(first & (head == c))
            def _(h=h, c=c):
                x_copy(g, h, c).wait_send()

            @pl.when(first & (head == h))
            def _(h=h, c=c):
                y_copy(g, h, c).wait_send()
        return carry

    lax.fori_loop(0, G, drain, 0)


def shards(head_count, seq_count, queries, keys, values, output_gradient, windows, sinks):
    G, D, T = KEY_VALUE_HEADS, HEAD_DIMENSION, BLOCK_TOKENS
    assert queries.shape[1] == T
    bf16, f32 = jnp.bfloat16, jnp.float32
    dma = pltpu.SemaphoreType.DMA
    vmem = pl.BlockSpec(memory_space=pltpu.VMEM)
    smem = pl.BlockSpec(memory_space=pltpu.SMEM)
    dq, dk, dv = pl.pallas_call(
        functools.partial(kernel, head_count, seq_count),
        out_shape=(
            jax.ShapeDtypeStruct((T, QUERY_HEADS * D), bf16),
            jax.ShapeDtypeStruct((T, G * D), bf16),
            jax.ShapeDtypeStruct((T, G * D), bf16),
        ),
        in_specs=[pl.BlockSpec(memory_space=pltpu.HBM)] * 4 + [smem] * 2,
        out_specs=(vmem,) * 3,
        scratch_shapes=[
            pltpu.VMEM((T, QUERY_HEADS * D), bf16),
            pltpu.VMEM((T, QUERY_HEADS * D), bf16),
            pltpu.VMEM(((WMAX + SMAX) * T, GROUP * T), f32),
            pltpu.VMEM(((WMAX + SMAX) * T, GROUP * T), f32),
            pltpu.VMEM(((WMAX + SMAX) * T, GROUP * T), bf16),
            pltpu.VMEM(((WMAX + SMAX) * T, GROUP * T), bf16),
            pltpu.VMEM((G, 2, T, D), bf16),
            pltpu.VMEM((G, BACK, 2, T, D), bf16),
            pltpu.VMEM((G, SMAX, 2, T, D), bf16),
            pltpu.VMEM((G, BACK, 2, T, D), bf16),
            pltpu.VMEM((G, BACK, 2, T, D), bf16),
            pltpu.VMEM((G, SMAX, 2, T, D), bf16),
            pltpu.VMEM((G, 2, SMAX, 2, T, D), bf16),
            pltpu.VMEM((G, 2, T, D), f32),
            pltpu.VMEM((G, SMAX, 2, T, D), f32),
            pltpu.VMEM((head_count, G, 2, T, D), bf16),
            dma((G, BACK)), dma((G, BACK)),
            dma((G, 2)), dma((G,)),
            dma((G, head_count)), dma((G, SMAX)),
            dma((G, BACK)), dma((G, BACK)),
            dma((G,)), dma((G, 2)),
            dma((G, SMAX)), dma((head_count, G)), dma((G, 4)),
        ],
        compiler_params=pltpu.CompilerParams(
            collective_id=0, has_side_effects=True, vmem_limit_bytes=58 * 2**20),
    )(queries[0], keys[0], values[0], output_gradient[0], windows, sinks)
    return dq[None], dk[None], dv[None]


def solution(mesh):
    return jax.shard_map(
        functools.partial(shards, mesh.shape["head"], mesh.shape["seq"]),
        mesh=mesh,
        in_specs=(
            P("seq", "head", None),
            P("seq", "head", None),
            P("seq", "head", None),
            P("seq", "head", None),
            P(),
            P(),
        ),
        out_specs=(P("seq", "head", None), P("seq", "head", None), P("seq", "head", None)),
        check_vma=False,
    )
```

```python
import functools
import math

import jax
import jax.numpy as jnp
from jax import lax
from jax.experimental import pallas as pl
from jax.experimental.pallas import tpu as pltpu
from jax.sharding import PartitionSpec as P

QUERY_HEADS = 32
KEY_VALUE_HEADS = 8
HEAD_DIMENSION = 128
BLOCK_TOKENS = 128
WMAX = 4
SMAX = 2

NEG_FILL = -1e30
GROUP = QUERY_HEADS // KEY_VALUE_HEADS
BACK = WMAX - 1
LOOK = 2
AHEAD = 4
MESH = pl.DeviceIdType.MESH


def spare_links(head_count):
    return [
        (h, c)
        for c in range(SMAX)
        for h in range(head_count)
        if h != c and not 1 <= h - c <= BACK
    ]


def kernel(
    head_count,
    seq_count,
    q_hbm, k_hbm, v_hbm, go_hbm, win_ref, sink_ref,
    dq_ref, dk_ref, dv_ref,
    q_ref, go_ref, sc, gw, wb, ds, own, window, sunk, gsend, grecv, rsend, rrecv, gown, rpart, yrecv,
    w_send, w_recv, s_send, s_recv, x_send, x_recv,
    g_send, g_recv, r_send, r_recv, y_send, y_recv, in_sem,
):
    G = KEY_VALUE_HEADS
    D = HEAD_DIMENSION
    T = BLOCK_TOKENS
    head = lax.axis_index("head")
    seq = lax.axis_index("seq")
    total = head_count * seq_count
    b = seq * head_count + head
    levels = max(1, (seq_count - 1).bit_length())
    to_child = [(lax.rem(seq, 2 << k) == 0) & (seq + (1 << k) < seq_count) for k in range(levels)]
    to_parent = [lax.rem(seq, 2 << k) == (1 << k) for k in range(levels)]
    height = sum(to_child[k].astype(jnp.int32) for k in range(levels))
    leaf = height == 0
    first = seq == 0
    scale = 1.0 / math.sqrt(D)
    spare = spare_links(head_count)

    def device(block):
        return {"head": lax.rem(block + total, total) % head_count,
                "seq": lax.div(lax.rem(block + total, total), head_count)}

    def in_seq(s):
        return {"head": head, "seq": lax.rem(s + seq_count, seq_count)}

    def in_first(h):
        return {"head": h, "seq": 0}

    def remote(src, dst, ssem, rsem, where):
        return pltpu.make_async_remote_copy(
            src_ref=src, dst_ref=dst, send_sem=ssem, recv_sem=rsem,
            device_id=where, device_id_type=MESH)

    partners = []
    for d in range(1, BACK + 1):
        partners.append((b + d < total, device(b + d)))
        partners.append((b >= d, device(b - d)))
    for k in range(levels):
        partners.append((to_child[k], in_seq(seq + (1 << k))))
        partners.append((to_parent[k], in_seq(seq - (1 << k))))
    for h, c in spare:
        partners.append((first & (head == h), in_first(c)))
        partners.append((first & (head == c), in_first(h)))

    def kv_copies(g):
        cols = pl.ds(pl.multiple_of(g * D, D), D)
        return (pltpu.make_async_copy(k_hbm.at[:, cols], own.at[g, 0], in_sem.at[g, 0]),
                pltpu.make_async_copy(v_hbm.at[:, cols], own.at[g, 1], in_sem.at[g, 1]))

    def q_copies(g):
        cols = pl.ds(pl.multiple_of(g * GROUP * D, GROUP * D), GROUP * D)
        return (pltpu.make_async_copy(q_hbm.at[:, cols], q_ref.at[:, cols], in_sem.at[g, 2]),
                pltpu.make_async_copy(go_hbm.at[:, cols], go_ref.at[:, cols], in_sem.at[g, 3]))

    def load_kv(g, carry):
        for copy in kv_copies(g):
            copy.start()
        return carry

    def load_q(g, carry):
        for copy in q_copies(g):
            copy.start()
        return carry

    lax.fori_loop(0, G, load_kv, 0)
    lax.fori_loop(0, G, load_q, 0)

    barrier = pltpu.get_barrier_semaphore()
    expected = jnp.int32(0)
    for holds, where in partners:
        @pl.when(holds)
        def _(where=where):
            pl.semaphore_signal(barrier, inc=1, device_id=where, device_id_type=MESH)
        expected = expected + holds.astype(jnp.int32)

    for d in range(1, BACK + 1):
        @pl.when(b < d)
        def _(d=d):
            for g in range(G):
                window[g, d - 1] = jnp.zeros((2, T, D), jnp.bfloat16)

    pl.semaphore_wait(barrier, expected)

    def w_copy(g, d):
        return remote(own.at[g], window.at[g, d - 1], w_send.at[g, d - 1], w_recv.at[g, d - 1], device(b + d))

    def s_copy(g, k):
        return remote(sunk.at[g], sunk.at[g], s_send.at[g, k], s_recv.at[g], in_seq(seq + (1 << k)))

    def x_copy(g, h, c):
        return remote(own.at[g], sunk.at[g, c], x_send.at[g, h], x_recv.at[g, c], in_first(h))

    def g_copy(g, d):
        return remote(gsend.at[g, d - 1], grecv.at[g, d - 1], g_send.at[g, d - 1], g_recv.at[g, d - 1], device(b - d))

    def r_copy(g, k):
        return remote(rsend.at[g], rrecv.at[g, k], r_send.at[g], r_recv.at[g, k], in_seq(seq - (1 << k)))

    def y_copy(g, h, c):
        return remote(rsend.at[g, c], yrecv.at[h, g], y_send.at[g, c], y_recv.at[h, g], in_first(c))

    def start_sends(g, carry):
        for copy in kv_copies(g):
            copy.wait()
        for d in range(1, BACK + 1):
            @pl.when(b + d < total)
            def _(d=d):
                w_copy(g, d).start()
        for h, c in spare:
            @pl.when(first & (head == c))
            def _(h=h, c=c):
                x_copy(g, h, c).start()
        return carry

    lax.fori_loop(0, AHEAD, start_sends, 0)

    def wait_window(g):
        for d in range(1, BACK + 1):
            @pl.when(b >= d)
            def _(d=d):
                w_copy(g, d).wait_recv()

    def arrive(g):
        @pl.when(first)
        def _():
            wait_window(g)
            for c in range(SMAX):
                @pl.when(head == c)
                def _(c=c):
                    sunk[g, c] = own[g]
                for d in range(1, BACK + 1):
                    @pl.when(head == c + d)
                    def _(c=c, d=d):
                        sunk[g, c] = window[g, d - 1]
            for h, c in spare:
                @pl.when(head == h)
                def _(h=h, c=c):
                    x_copy(g, h, c).wait_recv()

        @pl.when(seq > 0)
        def _():
            s_copy(g, 0).wait_recv()

        for k in reversed(range(levels)):
            @pl.when(to_child[k])
            def _(k=k):
                s_copy(g, k).start()

    causal = lax.broadcasted_iota(jnp.int32, (T, T), 0) <= lax.broadcasted_iota(jnp.int32, (T, T), 1)

    def compute(g):
        @pl.when(seq > 0)
        def _():
            wait_window(g)

        for copy in q_copies(g):
            copy.wait()

        def stacked(kind):
            return jnp.concatenate(
                [own[g, kind]] + [window[g, d, kind] for d in range(BACK)]
                + [sunk[g, c, kind] for c in range(SMAX)], 0)

        def columns(r):
            return pl.ds(pl.multiple_of((g * GROUP + r) * D, D), D)

        k_all = stacked(0)
        v_all = stacked(1)
        q_all = jnp.concatenate([q_ref[:, columns(r)] for r in range(GROUP)], 0)
        go_all = jnp.concatenate([go_ref[:, columns(r)] for r in range(GROUP)], 0)
        wide = jnp.concatenate([jnp.full((1, T), win_ref[g * GROUP + r], jnp.int32) for r in range(GROUP)], 1)
        depth = jnp.concatenate([jnp.full((1, T), sink_ref[g * GROUP + r], jnp.int32) for r in range(GROUP)], 1)
        contract = (((1,), (1,)), ((), ()))
        for part in range(2):
            lanes = slice(part * 2 * T, (part + 1) * 2 * T)
            sc[:, lanes] = lax.dot_general(
                k_all, q_all[lanes], contract, preferred_element_type=jnp.float32)
            gw[:, lanes] = lax.dot_general(
                v_all, go_all[lanes], contract, preferred_element_type=jnp.float32)
        slots = WMAX + SMAX
        k_turned = k_all.astype(jnp.float32).T.astype(jnp.bfloat16)
        folded = scale * math.log2(math.e)

        def softmax(r):
            lanes = slice(r * T, (r + 1) * T)
            bias = [jnp.zeros((1, T), jnp.float32)]
            for d in range(1, WMAX):
                bias.append(jnp.where((wide[:, lanes] > d) & (b >= d), 0.0, NEG_FILL))
            for c in range(SMAX):
                bias.append(jnp.where((depth[:, lanes] > c) & (wide[:, lanes] <= b - c), 0.0, NEG_FILL))

            def raw(n):
                tile = sc[n * T:(n + 1) * T, lanes]
                return jnp.where(causal, tile, NEG_FILL) if n == 0 else tile

            top = None
            for n in range(slots):
                high = jnp.max(raw(n), 0, keepdims=True) * folded + bias[n]
                top = high if top is None else jnp.maximum(top, high)
            mass = dot = None
            for n in range(slots):
                rows = slice(n * T, (n + 1) * T)
                e = jnp.exp2(raw(n) * folded + (bias[n] - top))
                sc[rows, lanes] = e
                mass_n = jnp.sum(e.reshape(T // 8, 8, T), 0)
                dot_n = jnp.sum((e * gw[rows, lanes]).reshape(T // 8, 8, T), 0)
                mass = mass_n if mass is None else mass + mass_n
                dot = dot_n if dot is None else dot + dot_n
            inv = 1.0 / jnp.sum(mass, 0, keepdims=True)
            row_dot = jnp.sum(dot, 0, keepdims=True) * inv
            for n in range(slots):
                rows = slice(n * T, (n + 1) * T)
                weights = sc[rows, lanes] * inv
                wb[rows, lanes] = weights.astype(jnp.bfloat16)
                ds[rows, lanes] = (weights * (gw[rows, lanes] - row_dot)).astype(jnp.bfloat16)

        natural = (((1,), (0,)), ((), ()))
        dk = dv = None
        for part in range(2):
            lanes = slice(part * 2 * T, (part + 1) * 2 * T)
            for r in range(2 * part, 2 * part + 2):
                softmax(r)
            dscore_b = ds[:, lanes]
            dk_n = lax.dot_general(dscore_b, q_all[lanes], natural, preferred_element_type=jnp.float32)
            dv_n = lax.dot_general(wb[:, lanes], go_all[lanes], natural, preferred_element_type=jnp.float32)
            dk = dk_n if dk is None else dk + dk_n
            dv = dv_n if dv is None else dv + dv_n
            dq_t = lax.dot_general(k_turned, dscore_b, natural, preferred_element_type=jnp.float32) * scale
            for r in range(2):
                dq_ref[:, columns(2 * part + r)] = dq_t[:, r * T:(r + 1) * T].T.astype(jnp.bfloat16)
        dk = dk * scale
        for c in range(SMAX):
            rows = slice((WMAX + c) * T, (WMAX + c + 1) * T)
            rpart[g, c, 0] = dk[rows]
            rpart[g, c, 1] = dv[rows]

        @pl.when(leaf & ~first)
        def _():
            rsend[g] = rpart[g].astype(jnp.bfloat16)

        for k in range(levels):
            @pl.when(leaf & to_parent[k])
            def _(k=k):
                r_copy(g, k).start()

        for d in range(1, WMAX):
            rows = slice(d * T, (d + 1) * T)
            gsend[g, d - 1, 0] = dk[rows].astype(jnp.bfloat16)
            gsend[g, d - 1, 1] = dv[rows].astype(jnp.bfloat16)
            later = first & (head >= d) & (head < d + SMAX)

            @pl.when((b >= d) & ~later)
            def _(d=d):
                g_copy(g, d).start()
        gown[g, 0] = dk[:T]
        gown[g, 1] = dv[:T]

    def reduce(g):
        for k in range(levels):
            @pl.when(to_child[k])
            def _(k=k):
                r_copy(g, k).wait_recv()
                rpart[g] = rpart[g] + rrecv[g, k].astype(jnp.float32)

        for k in range(levels):
            @pl.when(to_parent[k])
            def _(k=k):
                rsend[g] = rpart[g].astype(jnp.bfloat16)
                r_copy(g, k).start()

        @pl.when(first)
        def _():
            for c in range(SMAX):
                @pl.when(head == c)
                def _(c=c):
                    gown[g] = gown[g] + rpart[g, c]
                for d in range(1, BACK + 1):
                    @pl.when(head == c + d)
                    def _(c=c, d=d):
                        gsend[g, d - 1] = (gsend[g, d - 1].astype(jnp.float32) + rpart[g, c]).astype(jnp.bfloat16)
                        g_copy(g, d).start()
            for h, c in spare:
                @pl.when(head == h)
                def _(h=h, c=c):
                    rsend[g, c] = rpart[g, c].astype(jnp.bfloat16)
                    y_copy(g, h, c).start()

    lag = jnp.clip(2 * height - 1, 0, G)

    def prologue(g, carry):
        arrive(g)
        return carry

    lax.fori_loop(0, LOOK, prologue, 0)

    def step(i, carry):
        @pl.when(i + AHEAD < G)
        def _():
            start_sends(i + AHEAD, 0)

        @pl.when(i + LOOK < G)
        def _():
            arrive(i + LOOK)

        @pl.when(i < G)
        def _():
            compute(i)

        j = i - lag

        @pl.when((first | ~leaf) & (j >= 0) & (j < G))
        def _():
            reduce(j)
        return carry

    lax.fori_loop(0, 2 * G, step, 0)

    def finish(g, carry):
        for d in range(1, BACK + 1):
            @pl.when(b + d < total)
            def _(d=d):
                g_copy(g, d).wait_recv()
                gown[g] = gown[g] + grecv[g, d - 1].astype(jnp.float32)
        for h, c in spare:
            @pl.when(first & (head == c))
            def _(h=h, c=c):
                y_copy(g, h, c).wait_recv()
                gown[g] = gown[g] + yrecv[h, g].astype(jnp.float32)
        cols = pl.ds(pl.multiple_of(g * D, D), D)
        dk_ref[:, cols] = gown[g, 0].astype(jnp.bfloat16)
        dv_ref[:, cols] = gown[g, 1].astype(jnp.bfloat16)
        return carry

    lax.fori_loop(0, G, finish, 0)

    def drain(g, carry):
        for d in range(1, BACK + 1):
            @pl.when(b + d < total)
            def _(d=d):
                w_copy(g, d).wait_send()

            @pl.when(b >= d)
            def _(d=d):
                g_copy(g, d).wait_send()

        for k in range(levels):
            @pl.when(to_child[k])
            def _(k=k):
                s_copy(g, k).wait_send()

            @pl.when(to_parent[k])
            def _(k=k):
                r_copy(g, k).wait_send()

        for h, c in spare:
            @pl.when(first & (head == c))
            def _(h=h, c=c):
                x_copy(g, h, c).wait_send()

            @pl.when(first & (head == h))
            def _(h=h, c=c):
                y_copy(g, h, c).wait_send()
        return carry

    lax.fori_loop(0, G, drain, 0)


def shards(head_count, seq_count, queries, keys, values, output_gradient, windows, sinks):
    G, D, T = KEY_VALUE_HEADS, HEAD_DIMENSION, BLOCK_TOKENS
    assert queries.shape[1] == T
    levels = max(1, (seq_count - 1).bit_length())
    bf16, f32 = jnp.bfloat16, jnp.float32
    dma = pltpu.SemaphoreType.DMA
    vmem = pl.BlockSpec(memory_space=pltpu.VMEM)
    smem = pl.BlockSpec(memory_space=pltpu.SMEM)
    dq, dk, dv = pl.pallas_call(
        functools.partial(kernel, head_count, seq_count),
        out_shape=(
            jax.ShapeDtypeStruct((T, QUERY_HEADS * D), bf16),
            jax.ShapeDtypeStruct((T, G * D), bf16),
            jax.ShapeDtypeStruct((T, G * D), bf16),
        ),
        in_specs=[pl.BlockSpec(memory_space=pltpu.HBM)] * 4 + [smem] * 2,
        out_specs=(vmem,) * 3,
        scratch_shapes=[
            pltpu.VMEM((T, QUERY_HEADS * D), bf16),
            pltpu.VMEM((T, QUERY_HEADS * D), bf16),
            pltpu.VMEM(((WMAX + SMAX) * T, GROUP * T), f32),
            pltpu.VMEM(((WMAX + SMAX) * T, GROUP * T), f32),
            pltpu.VMEM(((WMAX + SMAX) * T, GROUP * T), bf16),
            pltpu.VMEM(((WMAX + SMAX) * T, GROUP * T), bf16),
            pltpu.VMEM((G, 2, T, D), bf16),
            pltpu.VMEM((G, BACK, 2, T, D), bf16),
            pltpu.VMEM((G, SMAX, 2, T, D), bf16),
            pltpu.VMEM((G, BACK, 2, T, D), bf16),
            pltpu.VMEM((G, BACK, 2, T, D), bf16),
            pltpu.VMEM((G, SMAX, 2, T, D), bf16),
            pltpu.VMEM((G, levels, SMAX, 2, T, D), bf16),
            pltpu.VMEM((G, 2, T, D), f32),
            pltpu.VMEM((G, SMAX, 2, T, D), f32),
            pltpu.VMEM((head_count, G, 2, T, D), bf16),
            dma((G, BACK)), dma((G, BACK)),
            dma((G, levels)), dma((G,)),
            dma((G, head_count)), dma((G, SMAX)),
            dma((G, BACK)), dma((G, BACK)),
            dma((G,)), dma((G, levels)),
            dma((G, SMAX)), dma((head_count, G)), dma((G, 4)),
        ],
        compiler_params=pltpu.CompilerParams(
            collective_id=0, has_side_effects=True, vmem_limit_bytes=58 * 2**20),
    )(queries[0], keys[0], values[0], output_gradient[0], windows, sinks)
    return dq[None], dk[None], dv[None]


def solution(mesh):
    return jax.shard_map(
        functools.partial(shards, mesh.shape["head"], mesh.shape["seq"]),
        mesh=mesh,
        in_specs=(
            P("seq", "head", None),
            P("seq", "head", None),
            P("seq", "head", None),
            P("seq", "head", None),
            P(),
            P(),
        ),
        out_specs=(P("seq", "head", None), P("seq", "head", None), P("seq", "head", None)),
        check_vma=False,
    )
```

```python
import functools
import math

import jax
import jax.numpy as jnp
from jax import lax
from jax.experimental import pallas as pl
from jax.experimental.pallas import tpu as pltpu
from jax.sharding import PartitionSpec as P

QUERY_HEADS = 32
KEY_VALUE_HEADS = 8
HEAD_DIMENSION = 128
BLOCK_TOKENS = 128
WMAX = 4
SMAX = 2

NEG_FILL = -1e30
GROUP = QUERY_HEADS // KEY_VALUE_HEADS
BACK = WMAX - 1
LOOK = 2
AHEAD = 4
HOLD = 2
PAIRS = ((1, 3, 0, 0), (2, 3, 0, 1), (2, 1, 1, 0), (3, 1, 1, 1))
MESH = pl.DeviceIdType.MESH


def spare_links(head_count):
    return [
        (h, c)
        for c in range(SMAX)
        for h in range(head_count)
        if h != c and not 1 <= h - c <= BACK
    ]


def kernel(
    head_count,
    seq_count,
    q_hbm, k_hbm, v_hbm, go_hbm, win_ref, sink_ref,
    dq_ref, dk_ref, dv_ref,
    q_ref, go_ref, prel, sc, gw, wb, ds, own, window, sunk, gsend, grecv, rsend, rrecv, gown, rpart, yrecv,
    w_send, w_recv, s_send, s_recv, x_send, x_recv,
    g_send, g_recv, r_send, r_recv, y_send, y_recv, in_sem,
    f_send, p_send, p_recv,
):
    G = KEY_VALUE_HEADS
    D = HEAD_DIMENSION
    T = BLOCK_TOKENS
    head = lax.axis_index("head")
    seq = lax.axis_index("seq")
    total = head_count * seq_count
    b = seq * head_count + head
    levels = max(1, (seq_count - 1).bit_length())
    to_child = [(lax.rem(seq, 2 << k) == 0) & (seq + (1 << k) < seq_count) for k in range(levels)]
    to_parent = [lax.rem(seq, 2 << k) == (1 << k) for k in range(levels)]
    height = sum(to_child[k].astype(jnp.int32) for k in range(levels))
    leaf = height == 0
    first = seq == 0
    scale = 1.0 / math.sqrt(D)
    spare = spare_links(head_count)

    def device(block):
        return {"head": lax.rem(block + total, total) % head_count,
                "seq": lax.div(lax.rem(block + total, total), head_count)}

    def in_seq(s):
        return {"head": head, "seq": lax.rem(s + seq_count, seq_count)}

    def in_first(h):
        return {"head": h, "seq": 0}

    def remote(src, dst, ssem, rsem, where):
        return pltpu.make_async_remote_copy(
            src_ref=src, dst_ref=dst, send_sem=ssem, recv_sem=rsem,
            device_id=where, device_id_type=MESH)

    partners = []
    for d in range(1, BACK + 1):
        partners.append((b + d < total, device(b + d)))
        partners.append((b >= d, device(b - d)))
    for k in range(levels):
        partners.append((to_child[k], in_seq(seq + (1 << k))))
        partners.append((to_parent[k], in_seq(seq - (1 << k))))
    for h, c in spare:
        partners.append((first & (head == h), in_first(c)))
        partners.append((first & (head == c), in_first(h)))

    def kv_copies(g):
        cols = pl.ds(pl.multiple_of(g * D, D), D)
        return (pltpu.make_async_copy(k_hbm.at[:, cols], own.at[g, 0], in_sem.at[g, 0]),
                pltpu.make_async_copy(v_hbm.at[:, cols], own.at[g, 1], in_sem.at[g, 1]))

    def q_copies(g):
        cols = pl.ds(pl.multiple_of(g * GROUP * D, GROUP * D), GROUP * D)
        return (pltpu.make_async_copy(q_hbm.at[:, cols], q_ref.at[:, cols], in_sem.at[g, 2]),
                pltpu.make_async_copy(go_hbm.at[:, cols], go_ref.at[:, cols], in_sem.at[g, 3]))

    def load_kv(g, carry):
        for copy in kv_copies(g):
            copy.start()
        return carry

    def load_q(g, carry):
        for copy in q_copies(g):
            copy.start()
        return carry

    lax.fori_loop(0, G, load_kv, 0)
    lax.fori_loop(0, G, load_q, 0)

    barrier = pltpu.get_barrier_semaphore()
    expected = jnp.int32(0)
    for holds, where in partners:
        @pl.when(holds)
        def _(where=where):
            pl.semaphore_signal(barrier, inc=1, device_id=where, device_id_type=MESH)
        expected = expected + holds.astype(jnp.int32)

    for d in range(1, BACK + 1):
        @pl.when(b < d)
        def _(d=d):
            for g in range(G):
                window[g, d - 1] = jnp.zeros((2, T, D), jnp.bfloat16)

    pl.semaphore_wait(barrier, expected)

    def w_copy(g, d):
        return remote(own.at[g], window.at[g, d - 1], w_send.at[g, d - 1], w_recv.at[g, d - 1], device(b + d))

    def s_copy(g, k):
        return remote(sunk.at[g], sunk.at[g], s_send.at[g, k], s_recv.at[g], in_seq(seq + (1 << k)))

    def x_copy(g, h, c):
        return remote(own.at[g], sunk.at[g, c], x_send.at[g, h], x_recv.at[g, c], in_first(h))

    def g_copy(g, d):
        return remote(gsend.at[g, d - 1], grecv.at[g, d - 1], g_send.at[g, d - 1], g_recv.at[g, d - 1], device(b - d))

    def r_copy(g, k):
        return remote(rsend.at[g], rrecv.at[g, k], r_send.at[g], r_recv.at[g, k], in_seq(seq - (1 << k)))

    def y_copy(g, h, c):
        return remote(rsend.at[g, c], yrecv.at[h, g], y_send.at[g, c], y_recv.at[h, g], in_first(c))

    def relayed(block, g, pair):
        near, far, parity, turn = pair
        if head_count != 4:
            return jnp.bool_(False)
        return ((block >= SMAX) & (lax.rem(block + total, 2) == parity) & (lax.rem(g, 2) == turn)
                & (block + max(near, far) < total))

    def relayed_to(block, g, d):
        hit = jnp.bool_(False)
        for pair in PAIRS:
            if pair[1] == d:
                hit = hit | relayed(block, g, pair)
        return hit

    def passes(g, d):
        hit = jnp.bool_(False)
        for pair in PAIRS:
            if pair[0] == d:
                hit = hit | relayed(b - d, g, pair)
        return hit

    def f_copy(g, near, far):
        return remote(window.at[g, near - 1], window.at[g, far - 1], f_send.at[g, near - 1], w_recv.at[g, far - 1],
                      device(b + far - near))

    def p_copy(g, near, far):
        return remote(gsend.at[g, far - 1], prel.at[g, near - 1], p_send.at[g, far - 1], p_recv.at[g, near - 1],
                      device(b - far + near))

    def start_sends(g, carry):
        for copy in kv_copies(g):
            copy.wait()
        for d in range(1, BACK + 1):
            @pl.when((b + d < total) & ~relayed_to(b, g, d))
            def _(d=d):
                w_copy(g, d).start()
        for h, c in spare:
            @pl.when(first & (head == c))
            def _(h=h, c=c):
                x_copy(g, h, c).start()
        return carry

    lax.fori_loop(0, AHEAD, start_sends, 0)

    def wait_window(g):
        for d in range(1, BACK + 1):
            @pl.when((b >= d) & ~passes(g, d))
            def _(d=d):
                w_copy(g, d).wait_recv()

    def arrive(g):
        for pair in PAIRS:
            @pl.when(relayed(b - pair[0], g, pair))
            def _(near=pair[0], far=pair[1]):
                w_copy(g, near).wait_recv()
                f_copy(g, near, far).start()

        @pl.when(first)
        def _():
            wait_window(g)
            for c in range(SMAX):
                @pl.when(head == c)
                def _(c=c):
                    sunk[g, c] = own[g]
                for d in range(1, BACK + 1):
                    @pl.when(head == c + d)
                    def _(c=c, d=d):
                        sunk[g, c] = window[g, d - 1]
            for h, c in spare:
                @pl.when(head == h)
                def _(h=h, c=c):
                    x_copy(g, h, c).wait_recv()

        @pl.when(seq > 0)
        def _():
            s_copy(g, 0).wait_recv()

        for k in reversed(range(levels)):
            @pl.when(to_child[k])
            def _(k=k):
                s_copy(g, k).start()

    causal = lax.broadcasted_iota(jnp.int32, (T, T), 0) <= lax.broadcasted_iota(jnp.int32, (T, T), 1)

    def compute(g):
        @pl.when(seq > 0)
        def _():
            wait_window(g)

        for copy in q_copies(g):
            copy.wait()

        def stacked(kind):
            return jnp.concatenate(
                [own[g, kind]] + [window[g, d, kind] for d in range(BACK)]
                + [sunk[g, c, kind] for c in range(SMAX)], 0)

        def columns(r):
            return pl.ds(pl.multiple_of((g * GROUP + r) * D, D), D)

        k_all = stacked(0)
        v_all = stacked(1)
        q_all = jnp.concatenate([q_ref[:, columns(r)] for r in range(GROUP)], 0)
        go_all = jnp.concatenate([go_ref[:, columns(r)] for r in range(GROUP)], 0)
        wide = jnp.concatenate([jnp.full((1, T), win_ref[g * GROUP + r], jnp.int32) for r in range(GROUP)], 1)
        depth = jnp.concatenate([jnp.full((1, T), sink_ref[g * GROUP + r], jnp.int32) for r in range(GROUP)], 1)
        contract = (((1,), (1,)), ((), ()))
        for part in range(2):
            lanes = slice(part * 2 * T, (part + 1) * 2 * T)
            sc[:, lanes] = lax.dot_general(
                k_all, q_all[lanes], contract, preferred_element_type=jnp.float32)
            gw[:, lanes] = lax.dot_general(
                v_all, go_all[lanes], contract, preferred_element_type=jnp.float32)
        slots = WMAX + SMAX
        k_turned = k_all.astype(jnp.float32).T.astype(jnp.bfloat16)
        folded = scale * math.log2(math.e)

        def softmax(r):
            lanes = slice(r * T, (r + 1) * T)
            bias = [jnp.zeros((1, T), jnp.float32)]
            for d in range(1, WMAX):
                bias.append(jnp.where((wide[:, lanes] > d) & (b >= d), 0.0, NEG_FILL))
            for c in range(SMAX):
                bias.append(jnp.where((depth[:, lanes] > c) & (wide[:, lanes] <= b - c), 0.0, NEG_FILL))

            def raw(n):
                tile = sc[n * T:(n + 1) * T, lanes]
                return jnp.where(causal, tile, NEG_FILL) if n == 0 else tile

            top = None
            for n in range(slots):
                high = jnp.max(raw(n), 0, keepdims=True) * folded + bias[n]
                top = high if top is None else jnp.maximum(top, high)
            mass = dot = None
            for n in range(slots):
                rows = slice(n * T, (n + 1) * T)
                e = jnp.exp2(raw(n) * folded + (bias[n] - top))
                sc[rows, lanes] = e
                mass_n = jnp.sum(e.reshape(T // 8, 8, T), 0)
                dot_n = jnp.sum((e * gw[rows, lanes]).reshape(T // 8, 8, T), 0)
                mass = mass_n if mass is None else mass + mass_n
                dot = dot_n if dot is None else dot + dot_n
            inv = 1.0 / jnp.sum(mass, 0, keepdims=True)
            row_dot = jnp.sum(dot, 0, keepdims=True) * inv
            for n in range(slots):
                rows = slice(n * T, (n + 1) * T)
                weights = sc[rows, lanes] * inv
                wb[rows, lanes] = weights.astype(jnp.bfloat16)
                ds[rows, lanes] = (weights * (gw[rows, lanes] - row_dot)).astype(jnp.bfloat16)

        natural = (((1,), (0,)), ((), ()))
        dk = dv = None
        for part in range(2):
            lanes = slice(part * 2 * T, (part + 1) * 2 * T)
            for r in range(2 * part, 2 * part + 2):
                softmax(r)
            dscore_b = ds[:, lanes]
            dk_n = lax.dot_general(dscore_b, q_all[lanes], natural, preferred_element_type=jnp.float32)
            dv_n = lax.dot_general(wb[:, lanes], go_all[lanes], natural, preferred_element_type=jnp.float32)
            dk = dk_n if dk is None else dk + dk_n
            dv = dv_n if dv is None else dv + dv_n
            dq_t = lax.dot_general(k_turned, dscore_b, natural, preferred_element_type=jnp.float32) * scale
            for r in range(2):
                dq_ref[:, columns(2 * part + r)] = dq_t[:, r * T:(r + 1) * T].T.astype(jnp.bfloat16)
        dk = dk * scale
        for c in range(SMAX):
            rows = slice((WMAX + c) * T, (WMAX + c + 1) * T)
            rpart[g, c, 0] = dk[rows]
            rpart[g, c, 1] = dv[rows]

        @pl.when(leaf & ~first)
        def _():
            rsend[g] = rpart[g].astype(jnp.bfloat16)

        for k in range(levels):
            @pl.when(leaf & to_parent[k])
            def _(k=k):
                r_copy(g, k).start()

        for d in range(1, WMAX):
            rows = slice(d * T, (d + 1) * T)
            gsend[g, d - 1, 0] = dk[rows].astype(jnp.bfloat16)
            gsend[g, d - 1, 1] = dv[rows].astype(jnp.bfloat16)
            later = first & (head >= d) & (head < d + SMAX)

            @pl.when((b >= d) & ~later & ~relayed_to(b - d, g, d) & ~passes(g, d))
            def _(d=d):
                g_copy(g, d).start()

            for pair in PAIRS:
                if pair[1] == d:
                    @pl.when(relayed(b - d, g, pair))
                    def _(near=pair[0], far=pair[1]):
                        p_copy(g, near, far).start()
        gown[g, 0] = dk[:T]
        gown[g, 1] = dv[:T]

    def reduce(g):
        for k in range(levels):
            @pl.when(to_child[k])
            def _(k=k):
                r_copy(g, k).wait_recv()
                rpart[g] = rpart[g] + rrecv[g, k].astype(jnp.float32)

        for k in range(levels):
            @pl.when(to_parent[k])
            def _(k=k):
                rsend[g] = rpart[g].astype(jnp.bfloat16)
                r_copy(g, k).start()

        @pl.when(first)
        def _():
            for c in range(SMAX):
                @pl.when(head == c)
                def _(c=c):
                    gown[g] = gown[g] + rpart[g, c]
                for d in range(1, BACK + 1):
                    @pl.when(head == c + d)
                    def _(c=c, d=d):
                        gsend[g, d - 1] = (gsend[g, d - 1].astype(jnp.float32) + rpart[g, c]).astype(jnp.bfloat16)
                        g_copy(g, d).start()
            for h, c in spare:
                @pl.when(head == h)
                def _(h=h, c=c):
                    rsend[g, c] = rpart[g, c].astype(jnp.bfloat16)
                    y_copy(g, h, c).start()

    def merge(g):
        for d in range(1, BACK + 1):
            @pl.when(passes(g, d))
            def _(d=d):
                p_copy(g, d, d).wait_recv()
                gsend[g, d - 1] = (
                    gsend[g, d - 1].astype(jnp.float32) + prel[g, d - 1].astype(jnp.float32)
                ).astype(jnp.bfloat16)
                g_copy(g, d).start()

    lag = jnp.clip(2 * height - 1, 0, G)

    def prologue(g, carry):
        arrive(g)
        return carry

    lax.fori_loop(0, LOOK, prologue, 0)

    def step(i, carry):
        @pl.when(i + LOOK < G)
        def _():
            arrive(i + LOOK)

        @pl.when(i + AHEAD < G)
        def _():
            start_sends(i + AHEAD, 0)

        @pl.when(i < G)
        def _():
            compute(i)

        j = i - lag

        @pl.when((first | ~leaf) & (j >= 0) & (j < G))
        def _():
            reduce(j)

        @pl.when((i >= HOLD) & (i - HOLD < G))
        def _():
            merge(i - HOLD)
        return carry

    lax.fori_loop(0, 2 * G, step, 0)

    def finish(g, carry):
        for d in range(1, BACK + 1):
            @pl.when((b + d < total) & ~relayed_to(b, g, d))
            def _(d=d):
                g_copy(g, d).wait_recv()
                gown[g] = gown[g] + grecv[g, d - 1].astype(jnp.float32)
        for h, c in spare:
            @pl.when(first & (head == c))
            def _(h=h, c=c):
                y_copy(g, h, c).wait_recv()
                gown[g] = gown[g] + yrecv[h, g].astype(jnp.float32)
        cols = pl.ds(pl.multiple_of(g * D, D), D)
        dk_ref[:, cols] = gown[g, 0].astype(jnp.bfloat16)
        dv_ref[:, cols] = gown[g, 1].astype(jnp.bfloat16)
        return carry

    lax.fori_loop(0, G, finish, 0)

    def drain(g, carry):
        for d in range(1, BACK + 1):
            @pl.when((b + d < total) & ~relayed_to(b, g, d))
            def _(d=d):
                w_copy(g, d).wait_send()

            @pl.when((b >= d) & ~relayed_to(b - d, g, d))
            def _(d=d):
                g_copy(g, d).wait_send()

        for pair in PAIRS:
            @pl.when(relayed(b - pair[0], g, pair))
            def _(near=pair[0], far=pair[1]):
                f_copy(g, near, far).wait_send()

            @pl.when(relayed(b - pair[1], g, pair))
            def _(near=pair[0], far=pair[1]):
                p_copy(g, near, far).wait_send()

        for k in range(levels):
            @pl.when(to_child[k])
            def _(k=k):
                s_copy(g, k).wait_send()

            @pl.when(to_parent[k])
            def _(k=k):
                r_copy(g, k).wait_send()

        for h, c in spare:
            @pl.when(first & (head == c))
            def _(h=h, c=c):
                x_copy(g, h, c).wait_send()

            @pl.when(first & (head == h))
            def _(h=h, c=c):
                y_copy(g, h, c).wait_send()
        return carry

    lax.fori_loop(0, G, drain, 0)


def shards(head_count, seq_count, queries, keys, values, output_gradient, windows, sinks):
    G, D, T = KEY_VALUE_HEADS, HEAD_DIMENSION, BLOCK_TOKENS
    assert queries.shape[1] == T
    levels = max(1, (seq_count - 1).bit_length())
    bf16, f32 = jnp.bfloat16, jnp.float32
    dma = pltpu.SemaphoreType.DMA
    vmem = pl.BlockSpec(memory_space=pltpu.VMEM)
    smem = pl.BlockSpec(memory_space=pltpu.SMEM)
    dq, dk, dv = pl.pallas_call(
        functools.partial(kernel, head_count, seq_count),
        out_shape=(
            jax.ShapeDtypeStruct((T, QUERY_HEADS * D), bf16),
            jax.ShapeDtypeStruct((T, G * D), bf16),
            jax.ShapeDtypeStruct((T, G * D), bf16),
        ),
        in_specs=[pl.BlockSpec(memory_space=pltpu.HBM)] * 4 + [smem] * 2,
        out_specs=(vmem,) * 3,
        scratch_shapes=[
            pltpu.VMEM((T, QUERY_HEADS * D), bf16),
            pltpu.VMEM((T, QUERY_HEADS * D), bf16),
            pltpu.VMEM((G, BACK, 2, T, D), bf16),
            pltpu.VMEM(((WMAX + SMAX) * T, GROUP * T), f32),
            pltpu.VMEM(((WMAX + SMAX) * T, GROUP * T), f32),
            pltpu.VMEM(((WMAX + SMAX) * T, GROUP * T), bf16),
            pltpu.VMEM(((WMAX + SMAX) * T, GROUP * T), bf16),
            pltpu.VMEM((G, 2, T, D), bf16),
            pltpu.VMEM((G, BACK, 2, T, D), bf16),
            pltpu.VMEM((G, SMAX, 2, T, D), bf16),
            pltpu.VMEM((G, BACK, 2, T, D), bf16),
            pltpu.VMEM((G, BACK, 2, T, D), bf16),
            pltpu.VMEM((G, SMAX, 2, T, D), bf16),
            pltpu.VMEM((G, levels, SMAX, 2, T, D), bf16),
            pltpu.VMEM((G, 2, T, D), f32),
            pltpu.VMEM((G, SMAX, 2, T, D), f32),
            pltpu.VMEM((head_count, G, 2, T, D), bf16),
            dma((G, BACK)), dma((G, BACK)),
            dma((G, levels)), dma((G,)),
            dma((G, head_count)), dma((G, SMAX)),
            dma((G, BACK)), dma((G, BACK)),
            dma((G,)), dma((G, levels)),
            dma((G, SMAX)), dma((head_count, G)), dma((G, 4)),
            dma((G, BACK)), dma((G, BACK)), dma((G, BACK)),
        ],
        compiler_params=pltpu.CompilerParams(
            collective_id=0, has_side_effects=True, vmem_limit_bytes=58 * 2**20),
    )(queries[0], keys[0], values[0], output_gradient[0], windows, sinks)
    return dq[None], dk[None], dv[None]


def solution(mesh):
    return jax.shard_map(
        functools.partial(shards, mesh.shape["head"], mesh.shape["seq"]),
        mesh=mesh,
        in_specs=(
            P("seq", "head", None),
            P("seq", "head", None),
            P("seq", "head", None),
            P("seq", "head", None),
            P(),
            P(),
        ),
        out_specs=(P("seq", "head", None), P("seq", "head", None), P("seq", "head", None)),
        check_vma=False,
    )
```

```python
import functools
import math

import jax
import jax.numpy as jnp
from jax import lax
from jax.experimental import pallas as pl
from jax.experimental.pallas import tpu as pltpu
from jax.sharding import PartitionSpec as P

QUERY_HEADS = 32
KEY_VALUE_HEADS = 8
HEAD_DIMENSION = 128
BLOCK_TOKENS = 128
WMAX = 4
SMAX = 2

NEG_FILL = -1e30
GROUP = QUERY_HEADS // KEY_VALUE_HEADS
BACK = WMAX - 1
LOOK = 1
AHEAD = 3
HOLD = 3
PAIRS = ((1, 3, 0, 0), (2, 3, 0, 1), (2, 1, 1, 0), (3, 1, 1, 1))
MESH = pl.DeviceIdType.MESH


def spare_links(head_count):
    return [
        (h, c)
        for c in range(SMAX)
        for h in range(head_count)
        if h != c and not 1 <= h - c <= BACK
    ]


def kernel(
    head_count,
    seq_count,
    q_hbm, k_hbm, v_hbm, go_hbm, win_ref, sink_ref,
    dq_ref, dk_ref, dv_ref,
    q_ref, go_ref, prel, sc, gw, wb, ds, own, window, sunk, gsend, grecv, rsend, rrecv, gown, rpart, yrecv,
    w_send, w_recv, s_send, s_recv, x_send, x_recv,
    g_send, g_recv, r_send, r_recv, y_send, y_recv, in_sem,
    f_send, p_send, p_recv,
):
    G = KEY_VALUE_HEADS
    D = HEAD_DIMENSION
    T = BLOCK_TOKENS
    head = lax.axis_index("head")
    seq = lax.axis_index("seq")
    total = head_count * seq_count
    b = seq * head_count + head
    levels = max(1, (seq_count - 1).bit_length())
    to_child = [(lax.rem(seq, 2 << k) == 0) & (seq + (1 << k) < seq_count) for k in range(levels)]
    to_parent = [lax.rem(seq, 2 << k) == (1 << k) for k in range(levels)]
    height = sum(to_child[k].astype(jnp.int32) for k in range(levels))
    leaf = height == 0
    first = seq == 0
    scale = 1.0 / math.sqrt(D)
    spare = spare_links(head_count)

    def device(block):
        return {"head": lax.rem(block + total, total) % head_count,
                "seq": lax.div(lax.rem(block + total, total), head_count)}

    def in_seq(s):
        return {"head": head, "seq": lax.rem(s + seq_count, seq_count)}

    def in_first(h):
        return {"head": h, "seq": 0}

    def remote(src, dst, ssem, rsem, where):
        return pltpu.make_async_remote_copy(
            src_ref=src, dst_ref=dst, send_sem=ssem, recv_sem=rsem,
            device_id=where, device_id_type=MESH)

    partners = []
    for d in range(1, BACK + 1):
        partners.append((b + d < total, device(b + d)))
        partners.append((b >= d, device(b - d)))
    for k in range(levels):
        partners.append((to_child[k], in_seq(seq + (1 << k))))
        partners.append((to_parent[k], in_seq(seq - (1 << k))))
    for h, c in spare:
        partners.append((first & (head == h), in_first(c)))
        partners.append((first & (head == c), in_first(h)))

    def kv_copies(g):
        cols = pl.ds(pl.multiple_of(g * D, D), D)
        return (pltpu.make_async_copy(k_hbm.at[:, cols], own.at[g, 0], in_sem.at[g, 0]),
                pltpu.make_async_copy(v_hbm.at[:, cols], own.at[g, 1], in_sem.at[g, 1]))

    def q_copies(g):
        cols = pl.ds(pl.multiple_of(g * GROUP * D, GROUP * D), GROUP * D)
        return (pltpu.make_async_copy(q_hbm.at[:, cols], q_ref.at[:, cols], in_sem.at[g, 2]),
                pltpu.make_async_copy(go_hbm.at[:, cols], go_ref.at[:, cols], in_sem.at[g, 3]))

    def load_kv(g, carry):
        for copy in kv_copies(g):
            copy.start()
        return carry

    def load_q(g, carry):
        for copy in q_copies(g):
            copy.start()
        return carry

    lax.fori_loop(0, G, load_kv, 0)
    lax.fori_loop(0, G, load_q, 0)

    barrier = pltpu.get_barrier_semaphore()
    expected = jnp.int32(0)
    for holds, where in partners:
        @pl.when(holds)
        def _(where=where):
            pl.semaphore_signal(barrier, inc=1, device_id=where, device_id_type=MESH)
        expected = expected + holds.astype(jnp.int32)

    for d in range(1, BACK + 1):
        @pl.when(b < d)
        def _(d=d):
            for g in range(G):
                window[g, d - 1] = jnp.zeros((2, T, D), jnp.bfloat16)

    pl.semaphore_wait(barrier, expected)

    def w_copy(g, d):
        return remote(own.at[g], window.at[g, d - 1], w_send.at[g, d - 1], w_recv.at[g, d - 1], device(b + d))

    def s_copy(g, k):
        return remote(sunk.at[g], sunk.at[g], s_send.at[g, k], s_recv.at[g], in_seq(seq + (1 << k)))

    def x_copy(g, h, c):
        return remote(own.at[g], sunk.at[g, c], x_send.at[g, h], x_recv.at[g, c], in_first(h))

    def g_copy(g, d):
        return remote(gsend.at[g, d - 1], grecv.at[g, d - 1], g_send.at[g, d - 1], g_recv.at[g, d - 1], device(b - d))

    def r_copy(g, k):
        return remote(rsend.at[g], rrecv.at[g, k], r_send.at[g], r_recv.at[g, k], in_seq(seq - (1 << k)))

    def y_copy(g, h, c):
        return remote(rsend.at[g, c], yrecv.at[h, g], y_send.at[g, c], y_recv.at[h, g], in_first(c))

    def relayed(block, g, pair):
        near, far, parity, turn = pair
        if head_count != 4:
            return jnp.bool_(False)
        return ((block >= SMAX) & (lax.rem(block + total, 2) == parity) & (lax.rem(g, 2) == turn)
                & (block + max(near, far) < total))

    def relayed_to(block, g, d):
        hit = jnp.bool_(False)
        for pair in PAIRS:
            if pair[1] == d:
                hit = hit | relayed(block, g, pair)
        return hit

    def passes(g, d):
        hit = jnp.bool_(False)
        for pair in PAIRS:
            if pair[0] == d:
                hit = hit | relayed(b - d, g, pair)
        return hit

    def f_copy(g, near, far):
        return remote(window.at[g, near - 1], window.at[g, far - 1], f_send.at[g, near - 1], w_recv.at[g, far - 1],
                      device(b + far - near))

    def p_copy(g, near, far):
        return remote(gsend.at[g, far - 1], prel.at[g, near - 1], p_send.at[g, far - 1], p_recv.at[g, near - 1],
                      device(b - far + near))

    def start_sends(g, carry):
        for copy in kv_copies(g):
            copy.wait()
        for d in range(1, BACK + 1):
            @pl.when((b + d < total) & ~relayed_to(b, g, d))
            def _(d=d):
                w_copy(g, d).start()
        for h, c in spare:
            @pl.when(first & (head == c))
            def _(h=h, c=c):
                x_copy(g, h, c).start()
        return carry

    lax.fori_loop(0, AHEAD - 1, start_sends, 0)

    def wait_window(g):
        for d in range(1, BACK + 1):
            @pl.when((b >= d) & ~passes(g, d))
            def _(d=d):
                w_copy(g, d).wait_recv()

    def arrive(g):
        for pair in PAIRS:
            @pl.when(relayed(b - pair[0], g, pair))
            def _(near=pair[0], far=pair[1]):
                w_copy(g, near).wait_recv()
                f_copy(g, near, far).start()

        @pl.when(first)
        def _():
            wait_window(g)
            for c in range(SMAX):
                @pl.when(head == c)
                def _(c=c):
                    sunk[g, c] = own[g]
                for d in range(1, BACK + 1):
                    @pl.when(head == c + d)
                    def _(c=c, d=d):
                        sunk[g, c] = window[g, d - 1]
            for h, c in spare:
                @pl.when(head == h)
                def _(h=h, c=c):
                    x_copy(g, h, c).wait_recv()

        @pl.when(seq > 0)
        def _():
            s_copy(g, 0).wait_recv()

        for k in reversed(range(levels)):
            @pl.when(to_child[k])
            def _(k=k):
                s_copy(g, k).start()

    causal = lax.broadcasted_iota(jnp.int32, (T, T), 0) <= lax.broadcasted_iota(jnp.int32, (T, T), 1)

    def compute(g):
        @pl.when(seq > 0)
        def _():
            wait_window(g)

        for copy in q_copies(g):
            copy.wait()

        def stacked(kind):
            return jnp.concatenate(
                [own[g, kind]] + [window[g, d, kind] for d in range(BACK)]
                + [sunk[g, c, kind] for c in range(SMAX)], 0)

        def columns(r):
            return pl.ds(pl.multiple_of((g * GROUP + r) * D, D), D)

        k_all = stacked(0)
        v_all = stacked(1)
        q_all = jnp.concatenate([q_ref[:, columns(r)] for r in range(GROUP)], 0)
        go_all = jnp.concatenate([go_ref[:, columns(r)] for r in range(GROUP)], 0)
        wide = jnp.concatenate([jnp.full((1, T), win_ref[g * GROUP + r], jnp.int32) for r in range(GROUP)], 1)
        depth = jnp.concatenate([jnp.full((1, T), sink_ref[g * GROUP + r], jnp.int32) for r in range(GROUP)], 1)
        contract = (((1,), (1,)), ((), ()))
        for part in range(2):
            lanes = slice(part * 2 * T, (part + 1) * 2 * T)
            sc[:, lanes] = lax.dot_general(
                k_all, q_all[lanes], contract, preferred_element_type=jnp.float32)
            gw[:, lanes] = lax.dot_general(
                v_all, go_all[lanes], contract, preferred_element_type=jnp.float32)
        slots = WMAX + SMAX
        k_turned = k_all.astype(jnp.float32).T.astype(jnp.bfloat16)
        folded = scale * math.log2(math.e)

        def softmax(r):
            lanes = slice(r * T, (r + 1) * T)
            bias = [jnp.zeros((1, T), jnp.float32)]
            for d in range(1, WMAX):
                bias.append(jnp.where((wide[:, lanes] > d) & (b >= d), 0.0, NEG_FILL))
            for c in range(SMAX):
                bias.append(jnp.where((depth[:, lanes] > c) & (wide[:, lanes] <= b - c), 0.0, NEG_FILL))

            def raw(n):
                tile = sc[n * T:(n + 1) * T, lanes]
                return jnp.where(causal, tile, NEG_FILL) if n == 0 else tile

            top = None
            for n in range(slots):
                high = jnp.max(raw(n), 0, keepdims=True) * folded + bias[n]
                top = high if top is None else jnp.maximum(top, high)
            mass = dot = None
            for n in range(slots):
                rows = slice(n * T, (n + 1) * T)
                e = jnp.exp2(raw(n) * folded + (bias[n] - top))
                sc[rows, lanes] = e
                mass_n = jnp.sum(e.reshape(T // 8, 8, T), 0)
                dot_n = jnp.sum((e * gw[rows, lanes]).reshape(T // 8, 8, T), 0)
                mass = mass_n if mass is None else mass + mass_n
                dot = dot_n if dot is None else dot + dot_n
            inv = 1.0 / jnp.sum(mass, 0, keepdims=True)
            row_dot = jnp.sum(dot, 0, keepdims=True) * inv
            for n in range(slots):
                rows = slice(n * T, (n + 1) * T)
                weights = sc[rows, lanes] * inv
                wb[rows, lanes] = weights.astype(jnp.bfloat16)
                ds[rows, lanes] = (weights * (gw[rows, lanes] - row_dot)).astype(jnp.bfloat16)

        natural = (((1,), (0,)), ((), ()))
        dk = dv = None
        for part in range(2):
            lanes = slice(part * 2 * T, (part + 1) * 2 * T)
            for r in range(2 * part, 2 * part + 2):
                softmax(r)
            dscore_b = ds[:, lanes]
            dk_n = lax.dot_general(dscore_b, q_all[lanes], natural, preferred_element_type=jnp.float32)
            dv_n = lax.dot_general(wb[:, lanes], go_all[lanes], natural, preferred_element_type=jnp.float32)
            dk = dk_n if dk is None else dk + dk_n
            dv = dv_n if dv is None else dv + dv_n
            dq_t = lax.dot_general(k_turned, dscore_b, natural, preferred_element_type=jnp.float32) * scale
            for r in range(2):
                dq_ref[:, columns(2 * part + r)] = dq_t[:, r * T:(r + 1) * T].T.astype(jnp.bfloat16)
        dk = dk * scale
        for c in range(SMAX):
            rows = slice((WMAX + c) * T, (WMAX + c + 1) * T)
            rpart[g, c, 0] = dk[rows]
            rpart[g, c, 1] = dv[rows]

        @pl.when(leaf & ~first)
        def _():
            rsend[g] = rpart[g].astype(jnp.bfloat16)

        for k in range(levels):
            @pl.when(leaf & to_parent[k])
            def _(k=k):
                r_copy(g, k).start()

        for d in range(1, WMAX):
            rows = slice(d * T, (d + 1) * T)
            gsend[g, d - 1, 0] = dk[rows].astype(jnp.bfloat16)
            gsend[g, d - 1, 1] = dv[rows].astype(jnp.bfloat16)
            later = first & (head >= d) & (head < d + SMAX)

            @pl.when((b >= d) & ~later & ~relayed_to(b - d, g, d) & ~passes(g, d))
            def _(d=d):
                g_copy(g, d).start()

            for pair in PAIRS:
                if pair[1] == d:
                    @pl.when(relayed(b - d, g, pair))
                    def _(near=pair[0], far=pair[1]):
                        p_copy(g, near, far).start()
        gown[g, 0] = dk[:T]
        gown[g, 1] = dv[:T]

    def reduce(g):
        for k in range(levels):
            @pl.when(to_child[k])
            def _(k=k):
                r_copy(g, k).wait_recv()
                rpart[g] = rpart[g] + rrecv[g, k].astype(jnp.float32)

        for k in range(levels):
            @pl.when(to_parent[k])
            def _(k=k):
                rsend[g] = rpart[g].astype(jnp.bfloat16)
                r_copy(g, k).start()

        @pl.when(first)
        def _():
            for c in range(SMAX):
                @pl.when(head == c)
                def _(c=c):
                    gown[g] = gown[g] + rpart[g, c]
                for d in range(1, BACK + 1):
                    @pl.when(head == c + d)
                    def _(c=c, d=d):
                        gsend[g, d - 1] = (gsend[g, d - 1].astype(jnp.float32) + rpart[g, c]).astype(jnp.bfloat16)
                        g_copy(g, d).start()
            for h, c in spare:
                @pl.when(head == h)
                def _(h=h, c=c):
                    rsend[g, c] = rpart[g, c].astype(jnp.bfloat16)
                    y_copy(g, h, c).start()

    def merge(g):
        for d in range(1, BACK + 1):
            @pl.when(passes(g, d))
            def _(d=d):
                p_copy(g, d, d).wait_recv()
                gsend[g, d - 1] = (
                    gsend[g, d - 1].astype(jnp.float32) + prel[g, d - 1].astype(jnp.float32)
                ).astype(jnp.bfloat16)
                g_copy(g, d).start()

    lag = jnp.clip(2 * height, 0, G)

    def prologue(g, carry):
        arrive(g)
        return carry

    lax.fori_loop(0, LOOK, prologue, 0)
    start_sends(AHEAD - 1, 0)

    def step(i, carry):
        @pl.when(i + LOOK < G)
        def _():
            arrive(i + LOOK)

        @pl.when(i + AHEAD < G)
        def _():
            start_sends(i + AHEAD, 0)

        @pl.when(i < G)
        def _():
            compute(i)

        j = i - lag

        @pl.when((first | ~leaf) & (j >= 0) & (j < G))
        def _():
            reduce(j)

        @pl.when((i >= HOLD) & (i - HOLD < G))
        def _():
            merge(i - HOLD)
        return carry

    lax.fori_loop(0, 2 * G, step, 0)

    def finish(g, carry):
        for d in range(1, BACK + 1):
            @pl.when((b + d < total) & ~relayed_to(b, g, d))
            def _(d=d):
                g_copy(g, d).wait_recv()
                gown[g] = gown[g] + grecv[g, d - 1].astype(jnp.float32)
        for h, c in spare:
            @pl.when(first & (head == c))
            def _(h=h, c=c):
                y_copy(g, h, c).wait_recv()
                gown[g] = gown[g] + yrecv[h, g].astype(jnp.float32)
        cols = pl.ds(pl.multiple_of(g * D, D), D)
        dk_ref[:, cols] = gown[g, 0].astype(jnp.bfloat16)
        dv_ref[:, cols] = gown[g, 1].astype(jnp.bfloat16)
        return carry

    lax.fori_loop(0, G, finish, 0)

    def drain(g, carry):
        for d in range(1, BACK + 1):
            @pl.when((b + d < total) & ~relayed_to(b, g, d))
            def _(d=d):
                w_copy(g, d).wait_send()

            @pl.when((b >= d) & ~relayed_to(b - d, g, d))
            def _(d=d):
                g_copy(g, d).wait_send()

        for pair in PAIRS:
            @pl.when(relayed(b - pair[0], g, pair))
            def _(near=pair[0], far=pair[1]):
                f_copy(g, near, far).wait_send()

            @pl.when(relayed(b - pair[1], g, pair))
            def _(near=pair[0], far=pair[1]):
                p_copy(g, near, far).wait_send()

        for k in range(levels):
            @pl.when(to_child[k])
            def _(k=k):
                s_copy(g, k).wait_send()

            @pl.when(to_parent[k])
            def _(k=k):
                r_copy(g, k).wait_send()

        for h, c in spare:
            @pl.when(first & (head == c))
            def _(h=h, c=c):
                x_copy(g, h, c).wait_send()

            @pl.when(first & (head == h))
            def _(h=h, c=c):
                y_copy(g, h, c).wait_send()
        return carry

    lax.fori_loop(0, G, drain, 0)


def shards(head_count, seq_count, queries, keys, values, output_gradient, windows, sinks):
    G, D, T = KEY_VALUE_HEADS, HEAD_DIMENSION, BLOCK_TOKENS
    assert queries.shape[1] == T
    levels = max(1, (seq_count - 1).bit_length())
    bf16, f32 = jnp.bfloat16, jnp.float32
    dma = pltpu.SemaphoreType.DMA
    vmem = pl.BlockSpec(memory_space=pltpu.VMEM)
    smem = pl.BlockSpec(memory_space=pltpu.SMEM)
    dq, dk, dv = pl.pallas_call(
        functools.partial(kernel, head_count, seq_count),
        out_shape=(
            jax.ShapeDtypeStruct((T, QUERY_HEADS * D), bf16),
            jax.ShapeDtypeStruct((T, G * D), bf16),
            jax.ShapeDtypeStruct((T, G * D), bf16),
        ),
        in_specs=[pl.BlockSpec(memory_space=pltpu.HBM)] * 4 + [smem] * 2,
        out_specs=(vmem,) * 3,
        scratch_shapes=[
            pltpu.VMEM((T, QUERY_HEADS * D), bf16),
            pltpu.VMEM((T, QUERY_HEADS * D), bf16),
            pltpu.VMEM((G, BACK, 2, T, D), bf16),
            pltpu.VMEM(((WMAX + SMAX) * T, GROUP * T), f32),
            pltpu.VMEM(((WMAX + SMAX) * T, GROUP * T), f32),
            pltpu.VMEM(((WMAX + SMAX) * T, GROUP * T), bf16),
            pltpu.VMEM(((WMAX + SMAX) * T, GROUP * T), bf16),
            pltpu.VMEM((G, 2, T, D), bf16),
            pltpu.VMEM((G, BACK, 2, T, D), bf16),
            pltpu.VMEM((G, SMAX, 2, T, D), bf16),
            pltpu.VMEM((G, BACK, 2, T, D), bf16),
            pltpu.VMEM((G, BACK, 2, T, D), bf16),
            pltpu.VMEM((G, SMAX, 2, T, D), bf16),
            pltpu.VMEM((G, levels, SMAX, 2, T, D), bf16),
            pltpu.VMEM((G, 2, T, D), f32),
            pltpu.VMEM((G, SMAX, 2, T, D), f32),
            pltpu.VMEM((head_count, G, 2, T, D), bf16),
            dma((G, BACK)), dma((G, BACK)),
            dma((G, levels)), dma((G,)),
            dma((G, head_count)), dma((G, SMAX)),
            dma((G, BACK)), dma((G, BACK)),
            dma((G,)), dma((G, levels)),
            dma((G, SMAX)), dma((head_count, G)), dma((G, 4)),
            dma((G, BACK)), dma((G, BACK)), dma((G, BACK)),
        ],
        compiler_params=pltpu.CompilerParams(
            collective_id=0, has_side_effects=True, vmem_limit_bytes=58 * 2**20),
    )(queries[0], keys[0], values[0], output_gradient[0], windows, sinks)
    return dq[None], dk[None], dv[None]


def solution(mesh):
    return jax.shard_map(
        functools.partial(shards, mesh.shape["head"], mesh.shape["seq"]),
        mesh=mesh,
        in_specs=(
            P("seq", "head", None),
            P("seq", "head", None),
            P("seq", "head", None),
            P("seq", "head", None),
            P(),
            P(),
        ),
        out_specs=(P("seq", "head", None), P("seq", "head", None), P("seq", "head", None)),
        check_vma=False,
    )
```

```python
import functools
import math

import jax
import jax.numpy as jnp
from jax import lax
from jax.experimental import pallas as pl
from jax.experimental.pallas import tpu as pltpu
from jax.sharding import PartitionSpec as P

QUERY_HEADS = 32
KEY_VALUE_HEADS = 8
HEAD_DIMENSION = 128
BLOCK_TOKENS = 128
WMAX = 4
SMAX = 2

NEG_FILL = -1e30
GROUP = QUERY_HEADS // KEY_VALUE_HEADS
BACK = WMAX - 1
LOOK = 3
AHEAD = 6
HOLD = 2
PAIRS = ((1, 3, 0, 0), (2, 3, 0, 1), (2, 1, 1, 0), (3, 1, 1, 1))
MESH = pl.DeviceIdType.MESH


def spare_links(head_count):
    return [
        (h, c)
        for c in range(SMAX)
        for h in range(head_count)
        if h != c and not 1 <= h - c <= BACK
    ]


def kernel(
    head_count,
    seq_count,
    q_hbm, k_hbm, v_hbm, go_hbm, win_ref, sink_ref,
    dq_ref, dk_ref, dv_ref,
    q_ref, go_ref, prel, sc, gw, wb, ds, own, window, sunk, gsend, grecv, rsend, rrecv, gown, rpart, yrecv,
    w_send, w_recv, s_send, s_recv, x_send, x_recv,
    g_send, g_recv, r_send, r_recv, y_send, y_recv, in_sem,
    f_send, p_send, p_recv,
):
    G = KEY_VALUE_HEADS
    D = HEAD_DIMENSION
    T = BLOCK_TOKENS
    head = lax.axis_index("head")
    seq = lax.axis_index("seq")
    total = head_count * seq_count
    b = seq * head_count + head
    levels = max(1, (seq_count - 1).bit_length())
    to_child = [(lax.rem(seq, 2 << k) == 0) & (seq + (1 << k) < seq_count) for k in range(levels)]
    to_parent = [lax.rem(seq, 2 << k) == (1 << k) for k in range(levels)]
    height = sum(to_child[k].astype(jnp.int32) for k in range(levels))
    leaf = height == 0
    first = seq == 0
    scale = 1.0 / math.sqrt(D)
    spare = spare_links(head_count)

    def device(block):
        return {"head": lax.rem(block + total, total) % head_count,
                "seq": lax.div(lax.rem(block + total, total), head_count)}

    def in_seq(s):
        return {"head": head, "seq": lax.rem(s + seq_count, seq_count)}

    def in_first(h):
        return {"head": h, "seq": 0}

    def remote(src, dst, ssem, rsem, where):
        return pltpu.make_async_remote_copy(
            src_ref=src, dst_ref=dst, send_sem=ssem, recv_sem=rsem,
            device_id=where, device_id_type=MESH)

    partners = []
    for d in range(1, BACK + 1):
        partners.append((b + d < total, device(b + d)))
        partners.append((b >= d, device(b - d)))
    for k in range(levels):
        partners.append((to_child[k], in_seq(seq + (1 << k))))
        partners.append((to_parent[k], in_seq(seq - (1 << k))))
    for h, c in spare:
        partners.append((first & (head == h), in_first(c)))
        partners.append((first & (head == c), in_first(h)))

    def kv_copies(g):
        cols = pl.ds(pl.multiple_of(g * D, D), D)
        return (pltpu.make_async_copy(k_hbm.at[:, cols], own.at[g, 0], in_sem.at[g, 0]),
                pltpu.make_async_copy(v_hbm.at[:, cols], own.at[g, 1], in_sem.at[g, 1]))

    def q_copies(g):
        cols = pl.ds(pl.multiple_of(g * GROUP * D, GROUP * D), GROUP * D)
        return (pltpu.make_async_copy(q_hbm.at[:, cols], q_ref.at[:, cols], in_sem.at[g, 2]),
                pltpu.make_async_copy(go_hbm.at[:, cols], go_ref.at[:, cols], in_sem.at[g, 3]))

    def load_kv(g, carry):
        for copy in kv_copies(g):
            copy.start()
        return carry

    def load_q(g, carry):
        for copy in q_copies(g):
            copy.start()
        return carry

    lax.fori_loop(0, G, load_kv, 0)
    lax.fori_loop(0, G, load_q, 0)

    barrier = pltpu.get_barrier_semaphore()
    expected = jnp.int32(0)
    for holds, where in partners:
        @pl.when(holds)
        def _(where=where):
            pl.semaphore_signal(barrier, inc=1, device_id=where, device_id_type=MESH)
        expected = expected + holds.astype(jnp.int32)

    for d in range(1, BACK + 1):
        @pl.when(b < d)
        def _(d=d):
            for g in range(G):
                window[g, d - 1] = jnp.zeros((2, T, D), jnp.bfloat16)

    pl.semaphore_wait(barrier, expected)

    def w_copy(g, d):
        return remote(own.at[g], window.at[g, d - 1], w_send.at[g, d - 1], w_recv.at[g, d - 1], device(b + d))

    def s_copy(g, k):
        return remote(sunk.at[g], sunk.at[g], s_send.at[g, k], s_recv.at[g], in_seq(seq + (1 << k)))

    def x_copy(g, h, c):
        return remote(own.at[g], sunk.at[g, c], x_send.at[g, h], x_recv.at[g, c], in_first(h))

    def g_copy(g, d):
        return remote(gsend.at[g, d - 1], grecv.at[g, d - 1], g_send.at[g, d - 1], g_recv.at[g, d - 1], device(b - d))

    def r_copy(g, k):
        return remote(rsend.at[g], rrecv.at[g, k], r_send.at[g], r_recv.at[g, k], in_seq(seq - (1 << k)))

    def y_copy(g, h, c):
        return remote(rsend.at[g, c], yrecv.at[h, g], y_send.at[g, c], y_recv.at[h, g], in_first(c))

    def relayed(block, g, pair):
        near, far, parity, turn = pair
        if head_count != 4:
            return jnp.bool_(False)
        return ((block >= SMAX) & (lax.rem(block + total, 2) == parity) & (lax.rem(g, 2) == turn)
                & (block + max(near, far) < total))

    def relayed_to(block, g, d):
        hit = jnp.bool_(False)
        for pair in PAIRS:
            if pair[1] == d:
                hit = hit | relayed(block, g, pair)
        return hit

    def passes(g, d):
        hit = jnp.bool_(False)
        for pair in PAIRS:
            if pair[0] == d:
                hit = hit | relayed(b - d, g, pair)
        return hit

    def f_copy(g, near, far):
        return remote(window.at[g, near - 1], window.at[g, far - 1], f_send.at[g, near - 1], w_recv.at[g, far - 1],
                      device(b + far - near))

    def p_copy(g, near, far):
        return remote(gsend.at[g, far - 1], prel.at[g, near - 1], p_send.at[g, far - 1], p_recv.at[g, near - 1],
                      device(b - far + near))

    def start_sends(g, carry):
        for copy in kv_copies(g):
            copy.wait()
        for d in range(1, BACK + 1):
            @pl.when((b + d < total) & ~relayed_to(b, g, d))
            def _(d=d):
                w_copy(g, d).start()
        for h, c in spare:
            @pl.when(first & (head == c))
            def _(h=h, c=c):
                x_copy(g, h, c).start()
        return carry

    lax.fori_loop(0, AHEAD, start_sends, 0)

    def wait_window(g):
        for d in range(1, BACK + 1):
            @pl.when((b >= d) & ~passes(g, d))
            def _(d=d):
                w_copy(g, d).wait_recv()

    def arrive(g):
        for pair in PAIRS:
            @pl.when(relayed(b - pair[0], g, pair))
            def _(near=pair[0], far=pair[1]):
                w_copy(g, near).wait_recv()
                f_copy(g, near, far).start()

        @pl.when(first)
        def _():
            wait_window(g)
            for c in range(SMAX):
                @pl.when(head == c)
                def _(c=c):
                    sunk[g, c] = own[g]
                for d in range(1, BACK + 1):
                    @pl.when(head == c + d)
                    def _(c=c, d=d):
                        sunk[g, c] = window[g, d - 1]
            for h, c in spare:
                @pl.when(head == h)
                def _(h=h, c=c):
                    x_copy(g, h, c).wait_recv()

        @pl.when(seq > 0)
        def _():
            s_copy(g, 0).wait_recv()

        for k in reversed(range(levels)):
            @pl.when(to_child[k])
            def _(k=k):
                s_copy(g, k).start()

    causal = lax.broadcasted_iota(jnp.int32, (T, T), 0) <= lax.broadcasted_iota(jnp.int32, (T, T), 1)

    def compute(g):
        @pl.when(seq > 0)
        def _():
            wait_window(g)

        for copy in q_copies(g):
            copy.wait()

        def stacked(kind):
            return jnp.concatenate(
                [own[g, kind]] + [window[g, d, kind] for d in range(BACK)]
                + [sunk[g, c, kind] for c in range(SMAX)], 0)

        def columns(r):
            return pl.ds(pl.multiple_of((g * GROUP + r) * D, D), D)

        k_all = stacked(0)
        v_all = stacked(1)
        q_all = jnp.concatenate([q_ref[:, columns(r)] for r in range(GROUP)], 0)
        go_all = jnp.concatenate([go_ref[:, columns(r)] for r in range(GROUP)], 0)
        wide = jnp.concatenate([jnp.full((1, T), win_ref[g * GROUP + r], jnp.int32) for r in range(GROUP)], 1)
        depth = jnp.concatenate([jnp.full((1, T), sink_ref[g * GROUP + r], jnp.int32) for r in range(GROUP)], 1)
        contract = (((1,), (1,)), ((), ()))
        for part in range(2):
            lanes = slice(part * 2 * T, (part + 1) * 2 * T)
            sc[:, lanes] = lax.dot_general(
                k_all, q_all[lanes], contract, preferred_element_type=jnp.float32)
            gw[:, lanes] = lax.dot_general(
                v_all, go_all[lanes], contract, preferred_element_type=jnp.float32)
        slots = WMAX + SMAX
        k_turned = k_all.astype(jnp.float32).T.astype(jnp.bfloat16)
        folded = scale * math.log2(math.e)

        def softmax(r):
            lanes = slice(r * T, (r + 1) * T)
            bias = [jnp.zeros((1, T), jnp.float32)]
            for d in range(1, WMAX):
                bias.append(jnp.where((wide[:, lanes] > d) & (b >= d), 0.0, NEG_FILL))
            for c in range(SMAX):
                bias.append(jnp.where((depth[:, lanes] > c) & (wide[:, lanes] <= b - c), 0.0, NEG_FILL))

            def raw(n):
                tile = sc[n * T:(n + 1) * T, lanes]
                return jnp.where(causal, tile, NEG_FILL) if n == 0 else tile

            top = None
            for n in range(slots):
                high = jnp.max(raw(n), 0, keepdims=True) * folded + bias[n]
                top = high if top is None else jnp.maximum(top, high)
            mass = dot = None
            for n in range(slots):
                rows = slice(n * T, (n + 1) * T)
                e = jnp.exp2(raw(n) * folded + (bias[n] - top))
                sc[rows, lanes] = e
                mass_n = jnp.sum(e.reshape(T // 8, 8, T), 0)
                dot_n = jnp.sum((e * gw[rows, lanes]).reshape(T // 8, 8, T), 0)
                mass = mass_n if mass is None else mass + mass_n
                dot = dot_n if dot is None else dot + dot_n
            inv = 1.0 / jnp.sum(mass, 0, keepdims=True)
            row_dot = jnp.sum(dot, 0, keepdims=True) * inv
            for n in range(slots):
                rows = slice(n * T, (n + 1) * T)
                weights = sc[rows, lanes] * inv
                wb[rows, lanes] = weights.astype(jnp.bfloat16)
                ds[rows, lanes] = (weights * (gw[rows, lanes] - row_dot)).astype(jnp.bfloat16)

        natural = (((1,), (0,)), ((), ()))
        dk = dv = None
        for part in range(2):
            lanes = slice(part * 2 * T, (part + 1) * 2 * T)
            for r in range(2 * part, 2 * part + 2):
                softmax(r)
            dscore_b = ds[:, lanes]
            dk_n = lax.dot_general(dscore_b, q_all[lanes], natural, preferred_element_type=jnp.float32)
            dv_n = lax.dot_general(wb[:, lanes], go_all[lanes], natural, preferred_element_type=jnp.float32)
            dk = dk_n if dk is None else dk + dk_n
            dv = dv_n if dv is None else dv + dv_n
            dq_t = lax.dot_general(k_turned, dscore_b, natural, preferred_element_type=jnp.float32) * scale
            for r in range(2):
                dq_ref[:, columns(2 * part + r)] = dq_t[:, r * T:(r + 1) * T].T.astype(jnp.bfloat16)
        dk = dk * scale
        for c in range(SMAX):
            rows = slice((WMAX + c) * T, (WMAX + c + 1) * T)
            rpart[g, c, 0] = dk[rows]
            rpart[g, c, 1] = dv[rows]

        @pl.when(leaf & ~first)
        def _():
            rsend[g] = rpart[g].astype(jnp.bfloat16)

        for k in range(levels):
            @pl.when(leaf & to_parent[k])
            def _(k=k):
                r_copy(g, k).start()

        for d in range(1, WMAX):
            rows = slice(d * T, (d + 1) * T)
            gsend[g, d - 1, 0] = dk[rows].astype(jnp.bfloat16)
            gsend[g, d - 1, 1] = dv[rows].astype(jnp.bfloat16)
            later = first & (head >= d) & (head < d + SMAX)

            @pl.when((b >= d) & ~later & ~relayed_to(b - d, g, d) & ~passes(g, d))
            def _(d=d):
                g_copy(g, d).start()

            for pair in PAIRS:
                if pair[1] == d:
                    @pl.when(relayed(b - d, g, pair))
                    def _(near=pair[0], far=pair[1]):
                        p_copy(g, near, far).start()
        gown[g, 0] = dk[:T]
        gown[g, 1] = dv[:T]

    def reduce(g):
        for k in range(levels):
            @pl.when(to_child[k])
            def _(k=k):
                r_copy(g, k).wait_recv()
                rpart[g] = rpart[g] + rrecv[g, k].astype(jnp.float32)

        for k in range(levels):
            @pl.when(to_parent[k])
            def _(k=k):
                rsend[g] = rpart[g].astype(jnp.bfloat16)
                r_copy(g, k).start()

        @pl.when(first)
        def _():
            for c in range(SMAX):
                @pl.when(head == c)
                def _(c=c):
                    gown[g] = gown[g] + rpart[g, c]
                for d in range(1, BACK + 1):
                    @pl.when(head == c + d)
                    def _(c=c, d=d):
                        gsend[g, d - 1] = (gsend[g, d - 1].astype(jnp.float32) + rpart[g, c]).astype(jnp.bfloat16)
                        g_copy(g, d).start()
            for h, c in spare:
                @pl.when(head == h)
                def _(h=h, c=c):
                    rsend[g, c] = rpart[g, c].astype(jnp.bfloat16)
                    y_copy(g, h, c).start()

    def merge(g):
        for d in range(1, BACK + 1):
            @pl.when(passes(g, d))
            def _(d=d):
                p_copy(g, d, d).wait_recv()
                gsend[g, d - 1] = (
                    gsend[g, d - 1].astype(jnp.float32) + prel[g, d - 1].astype(jnp.float32)
                ).astype(jnp.bfloat16)
                g_copy(g, d).start()

    lag = jnp.clip(2 * height - 1, 0, G)

    def prologue(g, carry):
        arrive(g)
        return carry

    lax.fori_loop(0, LOOK, prologue, 0)

    def step(i, carry):
        @pl.when(i + LOOK < G)
        def _():
            arrive(i + LOOK)

        @pl.when(i + AHEAD < G)
        def _():
            start_sends(i + AHEAD, 0)

        @pl.when(i < G)
        def _():
            compute(i)

        j = i - lag

        @pl.when((first | ~leaf) & (j >= 0) & (j < G))
        def _():
            reduce(j)

        @pl.when((i >= HOLD) & (i - HOLD < G))
        def _():
            merge(i - HOLD)
        return carry

    lax.fori_loop(0, 2 * G, step, 0)

    def finish(g, carry):
        for d in range(1, BACK + 1):
            @pl.when((b + d < total) & ~relayed_to(b, g, d))
            def _(d=d):
                g_copy(g, d).wait_recv()
                gown[g] = gown[g] + grecv[g, d - 1].astype(jnp.float32)
        for h, c in spare:
            @pl.when(first & (head == c))
            def _(h=h, c=c):
                y_copy(g, h, c).wait_recv()
                gown[g] = gown[g] + yrecv[h, g].astype(jnp.float32)
        cols = pl.ds(pl.multiple_of(g * D, D), D)
        dk_ref[:, cols] = gown[g, 0].astype(jnp.bfloat16)
        dv_ref[:, cols] = gown[g, 1].astype(jnp.bfloat16)
        return carry

    lax.fori_loop(0, G, finish, 0)

    def drain(g, carry):
        for d in range(1, BACK + 1):
            @pl.when((b + d < total) & ~relayed_to(b, g, d))
            def _(d=d):
                w_copy(g, d).wait_send()

            @pl.when((b >= d) & ~relayed_to(b - d, g, d))
            def _(d=d):
                g_copy(g, d).wait_send()

        for pair in PAIRS:
            @pl.when(relayed(b - pair[0], g, pair))
            def _(near=pair[0], far=pair[1]):
                f_copy(g, near, far).wait_send()

            @pl.when(relayed(b - pair[1], g, pair))
            def _(near=pair[0], far=pair[1]):
                p_copy(g, near, far).wait_send()

        for k in range(levels):
            @pl.when(to_child[k])
            def _(k=k):
                s_copy(g, k).wait_send()

            @pl.when(to_parent[k])
            def _(k=k):
                r_copy(g, k).wait_send()

        for h, c in spare:
            @pl.when(first & (head == c))
            def _(h=h, c=c):
                x_copy(g, h, c).wait_send()

            @pl.when(first & (head == h))
            def _(h=h, c=c):
                y_copy(g, h, c).wait_send()
        return carry

    lax.fori_loop(0, G, drain, 0)


def shards(head_count, seq_count, queries, keys, values, output_gradient, windows, sinks):
    G, D, T = KEY_VALUE_HEADS, HEAD_DIMENSION, BLOCK_TOKENS
    assert queries.shape[1] == T
    levels = max(1, (seq_count - 1).bit_length())
    bf16, f32 = jnp.bfloat16, jnp.float32
    dma = pltpu.SemaphoreType.DMA
    vmem = pl.BlockSpec(memory_space=pltpu.VMEM)
    smem = pl.BlockSpec(memory_space=pltpu.SMEM)
    dq, dk, dv = pl.pallas_call(
        functools.partial(kernel, head_count, seq_count),
        out_shape=(
            jax.ShapeDtypeStruct((T, QUERY_HEADS * D), bf16),
            jax.ShapeDtypeStruct((T, G * D), bf16),
            jax.ShapeDtypeStruct((T, G * D), bf16),
        ),
        in_specs=[pl.BlockSpec(memory_space=pltpu.HBM)] * 4 + [smem] * 2,
        out_specs=(vmem,) * 3,
        scratch_shapes=[
            pltpu.VMEM((T, QUERY_HEADS * D), bf16),
            pltpu.VMEM((T, QUERY_HEADS * D), bf16),
            pltpu.VMEM((G, BACK, 2, T, D), bf16),
            pltpu.VMEM(((WMAX + SMAX) * T, GROUP * T), f32),
            pltpu.VMEM(((WMAX + SMAX) * T, GROUP * T), f32),
            pltpu.VMEM(((WMAX + SMAX) * T, GROUP * T), bf16),
            pltpu.VMEM(((WMAX + SMAX) * T, GROUP * T), bf16),
            pltpu.VMEM((G, 2, T, D), bf16),
            pltpu.VMEM((G, BACK, 2, T, D), bf16),
            pltpu.VMEM((G, SMAX, 2, T, D), bf16),
            pltpu.VMEM((G, BACK, 2, T, D), bf16),
            pltpu.VMEM((G, BACK, 2, T, D), bf16),
            pltpu.VMEM((G, SMAX, 2, T, D), bf16),
            pltpu.VMEM((G, levels, SMAX, 2, T, D), bf16),
            pltpu.VMEM((G, 2, T, D), f32),
            pltpu.VMEM((G, SMAX, 2, T, D), f32),
            pltpu.VMEM((head_count, G, 2, T, D), bf16),
            dma((G, BACK)), dma((G, BACK)),
            dma((G, levels)), dma((G,)),
            dma((G, head_count)), dma((G, SMAX)),
            dma((G, BACK)), dma((G, BACK)),
            dma((G,)), dma((G, levels)),
            dma((G, SMAX)), dma((head_count, G)), dma((G, 4)),
            dma((G, BACK)), dma((G, BACK)), dma((G, BACK)),
        ],
        compiler_params=pltpu.CompilerParams(
            collective_id=0, has_side_effects=True, vmem_limit_bytes=58 * 2**20),
    )(queries[0], keys[0], values[0], output_gradient[0], windows, sinks)
    return dq[None], dk[None], dv[None]


def solution(mesh):
    return jax.shard_map(
        functools.partial(shards, mesh.shape["head"], mesh.shape["seq"]),
        mesh=mesh,
        in_specs=(
            P("seq", "head", None),
            P("seq", "head", None),
            P("seq", "head", None),
            P("seq", "head", None),
            P(),
            P(),
        ),
        out_specs=(P("seq", "head", None), P("seq", "head", None), P("seq", "head", None)),
        check_vma=False,
    )
```

```python
import functools
import math

import jax
import jax.numpy as jnp
from jax import lax
from jax.experimental import pallas as pl
from jax.experimental.pallas import tpu as pltpu
from jax.sharding import PartitionSpec as P

QUERY_HEADS = 32
KEY_VALUE_HEADS = 8
HEAD_DIMENSION = 128
BLOCK_TOKENS = 128
WMAX = 4
SMAX = 2

NEG_FILL = -1e30
GROUP = QUERY_HEADS // KEY_VALUE_HEADS
BACK = WMAX - 1
LOOK = 2
AHEAD = 4
HOLD = 2
PAIRS = ((1, 3, 0, 0), (2, 3, 0, 1), (2, 1, 1, 0), (3, 1, 1, 1))
MESH = pl.DeviceIdType.MESH


def spare_links(head_count):
    return [
        (h, c)
        for c in range(SMAX)
        for h in range(head_count)
        if h != c and not 1 <= h - c <= BACK
    ]


def kernel(
    head_count,
    seq_count,
    q_hbm, k_hbm, v_hbm, go_hbm, win_ref, sink_ref,
    dq_ref, dk_ref, dv_ref,
    q_ref, go_ref, prel, sc, gw, wb, ds, own, window, sunk, gsend, grecv, rsend, rrecv, gown, rpart, yrecv,
    w_send, w_recv, s_send, s_recv, x_send, x_recv,
    g_send, g_recv, r_send, r_recv, y_send, y_recv, in_sem,
    f_send, p_send, p_recv,
):
    G = KEY_VALUE_HEADS
    D = HEAD_DIMENSION
    T = BLOCK_TOKENS
    head = lax.axis_index("head")
    seq = lax.axis_index("seq")
    total = head_count * seq_count
    b = seq * head_count + head
    levels = max(1, (seq_count - 1).bit_length())
    to_child = [(lax.rem(seq, 2 << k) == 0) & (seq + (1 << k) < seq_count) for k in range(levels)]
    to_parent = [lax.rem(seq, 2 << k) == (1 << k) for k in range(levels)]
    height = sum(to_child[k].astype(jnp.int32) for k in range(levels))
    leaf = height == 0
    first = seq == 0
    scale = 1.0 / math.sqrt(D)
    spare = spare_links(head_count)

    def device(block):
        return {"head": lax.rem(block + total, total) % head_count,
                "seq": lax.div(lax.rem(block + total, total), head_count)}

    def in_seq(s):
        return {"head": head, "seq": lax.rem(s + seq_count, seq_count)}

    def in_first(h):
        return {"head": h, "seq": 0}

    def remote(src, dst, ssem, rsem, where):
        return pltpu.make_async_remote_copy(
            src_ref=src, dst_ref=dst, send_sem=ssem, recv_sem=rsem,
            device_id=where, device_id_type=MESH)

    partners = []
    for d in range(1, BACK + 1):
        partners.append((b + d < total, device(b + d)))
        partners.append((b >= d, device(b - d)))
    for k in range(levels):
        partners.append((to_child[k], in_seq(seq + (1 << k))))
        partners.append((to_parent[k], in_seq(seq - (1 << k))))
    for h, c in spare:
        partners.append((first & (head == h), in_first(c)))
        partners.append((first & (head == c), in_first(h)))

    def kv_copies(g):
        cols = pl.ds(pl.multiple_of(g * D, D), D)
        return (pltpu.make_async_copy(k_hbm.at[:, cols], own.at[g, 0], in_sem.at[g, 0]),
                pltpu.make_async_copy(v_hbm.at[:, cols], own.at[g, 1], in_sem.at[g, 1]))

    def q_copies(g):
        cols = pl.ds(pl.multiple_of(g * GROUP * D, GROUP * D), GROUP * D)
        return (pltpu.make_async_copy(q_hbm.at[:, cols], q_ref.at[:, cols], in_sem.at[g, 2]),
                pltpu.make_async_copy(go_hbm.at[:, cols], go_ref.at[:, cols], in_sem.at[g, 3]))

    def load_kv(g, carry):
        for copy in kv_copies(g):
            copy.start()
        return carry

    def load_q(g, carry):
        for copy in q_copies(g):
            copy.start()
        return carry

    lax.fori_loop(0, G, load_kv, 0)
    lax.fori_loop(0, G, load_q, 0)

    barrier = pltpu.get_barrier_semaphore()
    expected = jnp.int32(0)
    for holds, where in partners:
        @pl.when(holds)
        def _(where=where):
            pl.semaphore_signal(barrier, inc=1, device_id=where, device_id_type=MESH)
        expected = expected + holds.astype(jnp.int32)

    for d in range(1, BACK + 1):
        @pl.when(b < d)
        def _(d=d):
            for g in range(G):
                window[g, d - 1] = jnp.zeros((2, T, D), jnp.bfloat16)

    pl.semaphore_wait(barrier, expected)

    def w_copy(g, d):
        return remote(own.at[g], window.at[g, d - 1], w_send.at[g, d - 1], w_recv.at[g, d - 1], device(b + d))

    def s_copy(g, k):
        return remote(sunk.at[g], sunk.at[g], s_send.at[g, k], s_recv.at[g], in_seq(seq + (1 << k)))

    def x_copy(g, h, c):
        return remote(own.at[g], sunk.at[g, c], x_send.at[g, h], x_recv.at[g, c], in_first(h))

    def g_copy(g, d):
        return remote(gsend.at[g, d - 1], grecv.at[g, d - 1], g_send.at[g, d - 1], g_recv.at[g, d - 1], device(b - d))

    def r_copy(g, k):
        return remote(rsend.at[g], rrecv.at[g, k], r_send.at[g], r_recv.at[g, k], in_seq(seq - (1 << k)))

    def y_copy(g, h, c):
        return remote(rsend.at[g, c], yrecv.at[h, g], y_send.at[g, c], y_recv.at[h, g], in_first(c))

    def relayed(block, g, pair):
        near, far, parity, turn = pair
        if head_count != 4:
            return jnp.bool_(False)
        return ((block >= SMAX) & (lax.rem(block + total, 2) == parity) & (lax.rem(g, 2) == turn)
                & (block + max(near, far) < total))

    def relayed_to(block, g, d):
        hit = jnp.bool_(False)
        for pair in PAIRS:
            if pair[1] == d:
                hit = hit | relayed(block, g, pair)
        return hit

    def passes(g, d):
        hit = jnp.bool_(False)
        for pair in PAIRS:
            if pair[0] == d:
                hit = hit | relayed(b - d, g, pair)
        return hit

    def f_copy(g, near, far):
        return remote(window.at[g, near - 1], window.at[g, far - 1], f_send.at[g, near - 1], w_recv.at[g, far - 1],
                      device(b + far - near))

    def p_copy(g, near, far):
        return remote(gsend.at[g, far - 1], prel.at[g, near - 1], p_send.at[g, far - 1], p_recv.at[g, near - 1],
                      device(b - far + near))

    def start_sends(g, carry):
        for copy in kv_copies(g):
            copy.wait()
        for d in range(1, BACK + 1):
            @pl.when((b + d < total) & ~relayed_to(b, g, d))
            def _(d=d):
                w_copy(g, d).start()
        for h, c in spare:
            @pl.when(first & (head == c))
            def _(h=h, c=c):
                x_copy(g, h, c).start()
        return carry

    lax.fori_loop(0, AHEAD, start_sends, 0)

    def wait_window(g):
        for d in range(1, BACK + 1):
            @pl.when((b >= d) & ~passes(g, d))
            def _(d=d):
                w_copy(g, d).wait_recv()

    def arrive(g):
        for pair in PAIRS:
            @pl.when(relayed(b - pair[0], g, pair))
            def _(near=pair[0], far=pair[1]):
                w_copy(g, near).wait_recv()
                f_copy(g, near, far).start()

        @pl.when(first)
        def _():
            wait_window(g)
            for c in range(SMAX):
                @pl.when(head == c)
                def _(c=c):
                    sunk[g, c] = own[g]
                for d in range(1, BACK + 1):
                    @pl.when(head == c + d)
                    def _(c=c, d=d):
                        sunk[g, c] = window[g, d - 1]
            for h, c in spare:
                @pl.when(head == h)
                def _(h=h, c=c):
                    x_copy(g, h, c).wait_recv()

        @pl.when(seq > 0)
        def _():
            s_copy(g, 0).wait_recv()

        for k in reversed(range(levels)):
            @pl.when(to_child[k])
            def _(k=k):
                s_copy(g, k).start()

    causal = lax.broadcasted_iota(jnp.int32, (T, T), 0) <= lax.broadcasted_iota(jnp.int32, (T, T), 1)

    def compute(g):
        @pl.when(seq > 0)
        def _():
            wait_window(g)

        for copy in q_copies(g):
            copy.wait()

        def stacked(kind):
            return jnp.concatenate(
                [own[g, kind]] + [window[g, d, kind] for d in range(BACK)]
                + [sunk[g, c, kind] for c in range(SMAX)], 0)

        def columns(r):
            return pl.ds(pl.multiple_of((g * GROUP + r) * D, D), D)

        k_all = stacked(0)
        v_all = stacked(1)
        q_all = jnp.concatenate([q_ref[:, columns(r)] for r in range(GROUP)], 0)
        go_all = jnp.concatenate([go_ref[:, columns(r)] for r in range(GROUP)], 0)
        wide = jnp.concatenate([jnp.full((1, T), win_ref[g * GROUP + r], jnp.int32) for r in range(GROUP)], 1)
        depth = jnp.concatenate([jnp.full((1, T), sink_ref[g * GROUP + r], jnp.int32) for r in range(GROUP)], 1)
        contract = (((1,), (1,)), ((), ()))
        for part in range(2):
            lanes = slice(part * 2 * T, (part + 1) * 2 * T)
            sc[:, lanes] = lax.dot_general(
                k_all, q_all[lanes], contract, preferred_element_type=jnp.float32)
            gw[:, lanes] = lax.dot_general(
                v_all, go_all[lanes], contract, preferred_element_type=jnp.float32)
        slots = WMAX + SMAX
        k_turned = k_all.astype(jnp.float32).T.astype(jnp.bfloat16)
        folded = scale * math.log2(math.e)

        def softmax(r):
            lanes = slice(r * T, (r + 1) * T)
            bias = [jnp.zeros((1, T), jnp.float32)]
            for d in range(1, WMAX):
                bias.append(jnp.where((wide[:, lanes] > d) & (b >= d), 0.0, NEG_FILL))
            for c in range(SMAX):
                bias.append(jnp.where((depth[:, lanes] > c) & (wide[:, lanes] <= b - c), 0.0, NEG_FILL))

            def raw(n):
                tile = sc[n * T:(n + 1) * T, lanes]
                return jnp.where(causal, tile, NEG_FILL) if n == 0 else tile

            top = None
            for n in range(slots):
                high = jnp.max(raw(n), 0, keepdims=True) * folded + bias[n]
                top = high if top is None else jnp.maximum(top, high)
            mass = dot = None
            for n in range(slots):
                rows = slice(n * T, (n + 1) * T)
                e = jnp.exp2(raw(n) * folded + (bias[n] - top))
                sc[rows, lanes] = e
                mass_n = jnp.sum(e.reshape(T // 8, 8, T), 0)
                dot_n = jnp.sum((e * gw[rows, lanes]).reshape(T // 8, 8, T), 0)
                mass = mass_n if mass is None else mass + mass_n
                dot = dot_n if dot is None else dot + dot_n
            inv = 1.0 / jnp.sum(mass, 0, keepdims=True)
            row_dot = jnp.sum(dot, 0, keepdims=True) * inv
            for n in range(slots):
                rows = slice(n * T, (n + 1) * T)
                weights = sc[rows, lanes] * inv
                wb[rows, lanes] = weights.astype(jnp.bfloat16)
                ds[rows, lanes] = (weights * (gw[rows, lanes] - row_dot)).astype(jnp.bfloat16)

        natural = (((1,), (0,)), ((), ()))
        dk = dv = None
        for part in range(2):
            lanes = slice(part * 2 * T, (part + 1) * 2 * T)
            for r in range(2 * part, 2 * part + 2):
                softmax(r)
            dscore_b = ds[:, lanes]
            dk_n = lax.dot_general(dscore_b, q_all[lanes], natural, preferred_element_type=jnp.float32)
            dv_n = lax.dot_general(wb[:, lanes], go_all[lanes], natural, preferred_element_type=jnp.float32)
            dk = dk_n if dk is None else dk + dk_n
            dv = dv_n if dv is None else dv + dv_n
            dq_t = lax.dot_general(k_turned, dscore_b, natural, preferred_element_type=jnp.float32) * scale
            for r in range(2):
                dq_ref[:, columns(2 * part + r)] = dq_t[:, r * T:(r + 1) * T].T.astype(jnp.bfloat16)
        dk = dk * scale
        for c in range(SMAX):
            rows = slice((WMAX + c) * T, (WMAX + c + 1) * T)
            rpart[g, c, 0] = dk[rows]
            rpart[g, c, 1] = dv[rows]

        @pl.when(leaf & ~first)
        def _():
            rsend[g] = rpart[g].astype(jnp.bfloat16)

        for k in range(levels):
            @pl.when(leaf & to_parent[k])
            def _(k=k):
                r_copy(g, k).start()

        for d in range(1, WMAX):
            rows = slice(d * T, (d + 1) * T)
            gsend[g, d - 1, 0] = dk[rows].astype(jnp.bfloat16)
            gsend[g, d - 1, 1] = dv[rows].astype(jnp.bfloat16)
            later = first & (head >= d) & (head < d + SMAX)

            @pl.when((b >= d) & ~later & ~relayed_to(b - d, g, d) & ~passes(g, d))
            def _(d=d):
                g_copy(g, d).start()

            for pair in PAIRS:
                if pair[1] == d:
                    @pl.when(relayed(b - d, g, pair))
                    def _(near=pair[0], far=pair[1]):
                        p_copy(g, near, far).start()
        gown[g, 0] = dk[:T]
        gown[g, 1] = dv[:T]

    def reduce(g):
        for k in range(levels):
            @pl.when(to_child[k])
            def _(k=k):
                r_copy(g, k).wait_recv()
                rpart[g] = rpart[g] + rrecv[g, k].astype(jnp.float32)

        for k in range(levels):
            @pl.when(to_parent[k])
            def _(k=k):
                rsend[g] = rpart[g].astype(jnp.bfloat16)
                r_copy(g, k).start()

        @pl.when(first)
        def _():
            for c in range(SMAX):
                @pl.when(head == c)
                def _(c=c):
                    gown[g] = gown[g] + rpart[g, c]
                for d in range(1, BACK + 1):
                    @pl.when(head == c + d)
                    def _(c=c, d=d):
                        gsend[g, d - 1] = (gsend[g, d - 1].astype(jnp.float32) + rpart[g, c]).astype(jnp.bfloat16)
                        g_copy(g, d).start()
            for h, c in spare:
                @pl.when(head == h)
                def _(h=h, c=c):
                    rsend[g, c] = rpart[g, c].astype(jnp.bfloat16)
                    y_copy(g, h, c).start()

    def merge(g):
        for d in range(1, BACK + 1):
            @pl.when(passes(g, d))
            def _(d=d):
                p_copy(g, d, d).wait_recv()
                gsend[g, d - 1] = (
                    gsend[g, d - 1].astype(jnp.float32) + prel[g, d - 1].astype(jnp.float32)
                ).astype(jnp.bfloat16)
                g_copy(g, d).start()

    lag = jnp.clip(2 * height, 0, G)

    def prologue(g, carry):
        arrive(g)
        return carry

    lax.fori_loop(0, LOOK, prologue, 0)

    def step(i, carry):
        @pl.when(i + LOOK < G)
        def _():
            arrive(i + LOOK)

        @pl.when(i + AHEAD < G)
        def _():
            start_sends(i + AHEAD, 0)

        j = i - lag

        @pl.when((first | ~leaf) & (j >= 0) & (j < G))
        def _():
            reduce(j)

        @pl.when(i < G)
        def _():
            compute(i)

        @pl.when((i >= HOLD) & (i - HOLD < G))
        def _():
            merge(i - HOLD)
        return carry

    lax.fori_loop(0, 2 * G, step, 0)

    def finish(g, carry):
        for d in range(1, BACK + 1):
            @pl.when((b + d < total) & ~relayed_to(b, g, d))
            def _(d=d):
                g_copy(g, d).wait_recv()
                gown[g] = gown[g] + grecv[g, d - 1].astype(jnp.float32)
        for h, c in spare:
            @pl.when(first & (head == c))
            def _(h=h, c=c):
                y_copy(g, h, c).wait_recv()
                gown[g] = gown[g] + yrecv[h, g].astype(jnp.float32)
        cols = pl.ds(pl.multiple_of(g * D, D), D)
        dk_ref[:, cols] = gown[g, 0].astype(jnp.bfloat16)
        dv_ref[:, cols] = gown[g, 1].astype(jnp.bfloat16)
        return carry

    lax.fori_loop(0, G, finish, 0)

    def drain(g, carry):
        for d in range(1, BACK + 1):
            @pl.when((b + d < total) & ~relayed_to(b, g, d))
            def _(d=d):
                w_copy(g, d).wait_send()

            @pl.when((b >= d) & ~relayed_to(b - d, g, d))
            def _(d=d):
                g_copy(g, d).wait_send()

        for pair in PAIRS:
            @pl.when(relayed(b - pair[0], g, pair))
            def _(near=pair[0], far=pair[1]):
                f_copy(g, near, far).wait_send()

            @pl.when(relayed(b - pair[1], g, pair))
            def _(near=pair[0], far=pair[1]):
                p_copy(g, near, far).wait_send()

        for k in range(levels):
            @pl.when(to_child[k])
            def _(k=k):
                s_copy(g, k).wait_send()

            @pl.when(to_parent[k])
            def _(k=k):
                r_copy(g, k).wait_send()

        for h, c in spare:
            @pl.when(first & (head == c))
            def _(h=h, c=c):
                x_copy(g, h, c).wait_send()

            @pl.when(first & (head == h))
            def _(h=h, c=c):
                y_copy(g, h, c).wait_send()
        return carry

    lax.fori_loop(0, G, drain, 0)


def shards(head_count, seq_count, queries, keys, values, output_gradient, windows, sinks):
    G, D, T = KEY_VALUE_HEADS, HEAD_DIMENSION, BLOCK_TOKENS
    assert queries.shape[1] == T
    levels = max(1, (seq_count - 1).bit_length())
    bf16, f32 = jnp.bfloat16, jnp.float32
    dma = pltpu.SemaphoreType.DMA
    vmem = pl.BlockSpec(memory_space=pltpu.VMEM)
    smem = pl.BlockSpec(memory_space=pltpu.SMEM)
    dq, dk, dv = pl.pallas_call(
        functools.partial(kernel, head_count, seq_count),
        out_shape=(
            jax.ShapeDtypeStruct((T, QUERY_HEADS * D), bf16),
            jax.ShapeDtypeStruct((T, G * D), bf16),
            jax.ShapeDtypeStruct((T, G * D), bf16),
        ),
        in_specs=[pl.BlockSpec(memory_space=pltpu.HBM)] * 4 + [smem] * 2,
        out_specs=(vmem,) * 3,
        scratch_shapes=[
            pltpu.VMEM((T, QUERY_HEADS * D), bf16),
            pltpu.VMEM((T, QUERY_HEADS * D), bf16),
            pltpu.VMEM((G, BACK, 2, T, D), bf16),
            pltpu.VMEM(((WMAX + SMAX) * T, GROUP * T), f32),
            pltpu.VMEM(((WMAX + SMAX) * T, GROUP * T), f32),
            pltpu.VMEM(((WMAX + SMAX) * T, GROUP * T), bf16),
            pltpu.VMEM(((WMAX + SMAX) * T, GROUP * T), bf16),
            pltpu.VMEM((G, 2, T, D), bf16),
            pltpu.VMEM((G, BACK, 2, T, D), bf16),
            pltpu.VMEM((G, SMAX, 2, T, D), bf16),
            pltpu.VMEM((G, BACK, 2, T, D), bf16),
            pltpu.VMEM((G, BACK, 2, T, D), bf16),
            pltpu.VMEM((G, SMAX, 2, T, D), bf16),
            pltpu.VMEM((G, levels, SMAX, 2, T, D), bf16),
            pltpu.VMEM((G, 2, T, D), f32),
            pltpu.VMEM((G, SMAX, 2, T, D), f32),
            pltpu.VMEM((head_count, G, 2, T, D), bf16),
            dma((G, BACK)), dma((G, BACK)),
            dma((G, levels)), dma((G,)),
            dma((G, head_count)), dma((G, SMAX)),
            dma((G, BACK)), dma((G, BACK)),
            dma((G,)), dma((G, levels)),
            dma((G, SMAX)), dma((head_count, G)), dma((G, 4)),
            dma((G, BACK)), dma((G, BACK)), dma((G, BACK)),
        ],
        compiler_params=pltpu.CompilerParams(
            collective_id=0, has_side_effects=True, vmem_limit_bytes=58 * 2**20),
    )(queries[0], keys[0], values[0], output_gradient[0], windows, sinks)
    return dq[None], dk[None], dv[None]


def solution(mesh):
    return jax.shard_map(
        functools.partial(shards, mesh.shape["head"], mesh.shape["seq"]),
        mesh=mesh,
        in_specs=(
            P("seq", "head", None),
            P("seq", "head", None),
            P("seq", "head", None),
            P("seq", "head", None),
            P(),
            P(),
        ),
        out_specs=(P("seq", "head", None), P("seq", "head", None), P("seq", "head", None)),
        check_vma=False,
    )
```
